128 devices in a mesh: cuts: 2 (over x_hi), seq: 64 (over z, x_lo, y, core).
Axes of the slice: x: 4 (x_hi: 2, x_lo: 2; x = x_hi * 2 + x_lo), y: 4, z: 4, core: 2. Of those that a mesh axis runs over, the one named last changes fastest.
Arguments:
- values_in: bfloat16 [2, 65536, 2048], P('cuts', 'seq'), may hold values from -6 to 6
- gate_out: bfloat16 [2, 65536, 2048], P('cuts', 'seq'), may hold values from -6 to 6
- grad_out: bfloat16 [2, 65536, 2048], P('cuts', 'seq'), may hold values from -6 to 6
- left_factor: bfloat16 [256, 256, 256], P('seq'), may hold values from -0.375 to 0.375
- right_factor: bfloat16 [256, 256, 256], P('seq'), may hold values from -0.375 to 0.375
Outputs:
- grad_values: bfloat16 [2, 65536, 2048], P('cuts', 'seq')
- grad_gate: bfloat16 [2, 65536, 2048], P('cuts', 'seq')
- grad_left: float32 [256, 256, 256], P('seq')
- grad_right: float32 [256, 256, 256], P('seq')
The draws below stay inside these ranges and needn't reach their ends.
All inputs are finite; a program needn't handle non-finite values.
Results may differ from the reference program's by a relative error of at most 0.0057.
Values may be sent and summed in bfloat16 or wider, within the bound.
A program may use at most 128 MiB of HBM per device.

```python
import jax
import jax.numpy as jnp
from jax import lax

D = 2048
BLK = 256
SEQ = 65536
BATCH = 2


def shard_levels(own_key, dims, cuts, least, top_value):
    factor_of, own = 1.0, jax.random.fold_in(own_key, 6)
    for dim, shards_of in cuts:
        draws = jnp.exp(jax.random.uniform(jax.random.fold_in(own, dim), (shards_of,), jnp.float32, least / len(cuts), top_value / len(cuts)))
        factor_of = factor_of * jnp.repeat(draws, dims[dim] // shards_of).reshape([-1 if axis == dim else 1 for axis in range(len(dims))])
    return factor_of


def normal_values(stream_key, extent, scale, reach, cuts=(), dtype=jnp.bfloat16):
    values = scale * jax.random.normal(stream_key, extent, jnp.float32)
    if cuts:
        values = values * shard_levels(stream_key, extent, cuts, -0.22, 0.18)
    return jnp.clip(values, -reach, reach).astype(dtype)


def setup_inputs(seed: int = 0) -> dict:
    splits = jax.random.split(jax.random.key(seed), 6)
    return {
        "values_in": normal_values(splits[0], (BATCH, SEQ, D), 1.0, 6.0, ((0, 2), (1, 64))),
        "gate_out": normal_values(splits[1], (BATCH, SEQ, D), 1.0, 6.0, ((0, 2), (1, 64))),
        "grad_out": normal_values(splits[2], (BATCH, SEQ, D), 1.0, 6.0, ((0, 2), (1, 64))),
        "left_factor": normal_values(splits[3], (BLK, BLK, BLK), BLK ** -0.5, 0.375, ((0, 64),)),
        "right_factor": normal_values(splits[4], (BLK, BLK, BLK), BLK ** -0.5, 0.375, ((0, 64),)),
    }


def reference(values_in, gate_out, grad_out, left_factor, right_factor):
    left32 = left_factor.astype(jnp.float32)
    right32 = right_factor.astype(jnp.float32)

    def one_sequence(carry, items):
        values_one, gate_one, grad_one = items
        acc_left, acc_right = carry
        inputs = values_one.reshape(BLK, BLK, D).astype(jnp.float32)
        hidden = jnp.einsum("ikj,ijd->ikd", left32, inputs).astype(jnp.bfloat16)
        hidden32 = hidden.astype(jnp.float32)
        mixed = jnp.einsum("kmi,ikd->kmd", right32, hidden32)
        grad_rows = grad_one.reshape(BLK, BLK, D).astype(jnp.float32)
        gate_rows = gate_one.reshape(BLK, BLK, D).astype(jnp.float32)
        grad_gate = (grad_rows * mixed).astype(jnp.bfloat16).reshape(SEQ, D)
        grad_mixed = lax.optimization_barrier((grad_rows * gate_rows).astype(jnp.bfloat16)).astype(jnp.float32)
        part_right = jnp.einsum("kmd,ikd->kmi", grad_mixed, hidden32)
        grad_hidden = lax.optimization_barrier(jnp.einsum("kmi,kmd->ikd", right32, grad_mixed).astype(jnp.bfloat16)).astype(jnp.float32)
        grad_values = jnp.einsum("ikj,ikd->ijd", left32, grad_hidden).astype(jnp.bfloat16).reshape(SEQ, D)
        part_left = jnp.einsum("ikd,ijd->ikj", grad_hidden, inputs)
        return (acc_left + part_left, acc_right + part_right), (grad_values, grad_gate)

    start = (jnp.zeros((BLK, BLK, BLK), jnp.float32), jnp.zeros((BLK, BLK, BLK), jnp.float32))
    (grad_left, grad_right), (grad_values, grad_gate) = lax.scan(one_sequence, start, (values_in, gate_out, grad_out))
    return grad_values, grad_gate, grad_left, grad_right
```

```python
import functools

import jax
import jax.numpy as jnp
from jax import lax
from jax.experimental import pallas as pl
from jax.experimental.pallas import tpu as pltpu
from jax.sharding import PartitionSpec as P

MESH = pl.DeviceIdType.MESH
F32 = jnp.float32
BF16 = jnp.bfloat16
N = 64
OWN = 4
BLK = 256
D = 2048
ROWS = OWN * BLK
LANES = 512
NT = (((1,), (1,)), ((), ()))


def peer(me, step):
    quarter, turn, z = step // 16, (step // 4) % 4, step % 4
    y = (z + turn) % 4
    pair = (quarter + z + 2 * turn + turn // 2) % 4
    core = me % 2
    z = (z + core * (4 - 2 * z)) % 4
    y = (y + core * (4 - 2 * y)) % 4
    to_z = (me // 16 + z) % 4
    to_x = (me // 8 + pair) % 2
    to_y = (me // 2 + y) % 4
    to_core = (core + pair // 2) % 2
    return ((to_z * 2 + to_x) * 4 + to_y) * 2 + to_core


def kernel(a_hbm, g_hbm, dy_hbm, l_hbm, r_hbm,
           gv_hbm, gg_hbm, gl_hbm, gr_hbm,
           a, dz, dy, left, right, left_t, expand, perm, sent, got, sorted_, acc, part, part_in,
           in_sem, out_sem, send_sem, recv_sem, cut_send, cut_recv):
    cut = lax.axis_index("cuts")
    me = lax.axis_index("seq")
    other = 1 - cut
    half_d = D // 2

    barrier = pltpu.get_barrier_semaphore()

    def greet(step, _):
        pl.semaphore_signal(barrier, inc=1, device_id=(cut, peer(me, step)), device_id_type=MESH)
        return 0

    lax.fori_loop(1, N, greet, 0)
    pl.semaphore_signal(barrier, inc=1, device_id=(other, me), device_id_type=MESH)

    lo, hi = pl.ds(0, half_d), pl.ds(half_d, half_d)
    loads = [
        pltpu.make_async_copy(l_hbm, left, in_sem.at[0]),
        pltpu.make_async_copy(a_hbm.at[:, lo], a.at[:, lo], in_sem.at[1]),
        pltpu.make_async_copy(a_hbm.at[:, hi], a.at[:, hi], in_sem.at[2]),
        pltpu.make_async_copy(r_hbm, right, in_sem.at[3]),
        pltpu.make_async_copy(dy_hbm, dy, in_sem.at[4]),
        pltpu.make_async_copy(g_hbm, dz, in_sem.at[5]),
    ]
    for load in loads:
        load.start()

    rows = lax.broadcasted_iota(jnp.int32, (BLK, BLK), 0)
    cols = lax.broadcasted_iota(jnp.int32, (BLK, BLK), 1)

    def build_expand(which):
        factor = right if which else left
        own = (rows >> 1) & 3

        def body(n, _):
            half, group = n // 2, n % 2
            hit = cols == 4 * (32 * group + (rows >> 3)) + 2 * half + (rows & 1)
            for block in range(OWN):
                pick = jnp.where(hit & (own == block), 1.0, 0.0).astype(BF16)
                if which:
                    out = lax.dot_general(pick, factor[block], NT, preferred_element_type=F32)
                else:
                    out = jnp.dot(pick, factor[block], preferred_element_type=F32)
                expand[which, half, pl.ds(pl.multiple_of(group * BLK, BLK), BLK), pl.ds(block * BLK, BLK)] = out.astype(BF16)
            return 0

        lax.fori_loop(0, 4, body, 0)

    def compute(which, q):
        half, d0 = q // 2, (q % 2) * half_d
        source = dz if which else a

        def body(n, _):
            group, tile = n // 2, n % 2
            take = pl.ds(pl.multiple_of(group * BLK, BLK), BLK)
            factor = expand[which, half, take, :]
            outs = []
            for block in range(2):
                lanes = pl.ds(pl.multiple_of(d0 + block * LANES + tile * 256, 256), 256)
                out = jnp.dot(factor, source[:, lanes], preferred_element_type=F32)
                outs.append(out.reshape(32, 8, 256))
            out = jnp.concatenate(outs, axis=1).astype(BF16)
            sent[which, q, pl.ds(pl.multiple_of(group * 32, 32), 32), :, pl.ds(pl.multiple_of(tile * 256, 256), 256)] = out
            return 0

        lax.fori_loop(0, 4, body, 0)
        got[which, q, me] = sent[which, q, me]

    def send(which, q):
        def body(step, _):
            to = peer(me, step)
            pltpu.make_async_remote_copy(
                src_ref=sent.at[which, q, to], dst_ref=got.at[which, q, me],
                send_sem=send_sem.at[which, q], recv_sem=recv_sem.at[which, q],
                device_id=(cut, to), device_id_type=MESH,
            ).start()
            return 0

        lax.fori_loop(1, N, body, 0)

    def all_of(which, q):
        span = pl.ds(0, N - 1)
        return pltpu.make_async_remote_copy(
            src_ref=sent.at[which, q, span], dst_ref=got.at[which, q, span],
            send_sem=send_sem.at[which, q], recv_sem=recv_sem.at[which, q],
            device_id=(cut, me), device_id_type=MESH,
        )

    def receive(which, q):
        half, d0 = q // 2, (q % 2) * half_d
        all_of(which, q).wait_recv()

        def sort(group, _):
            x = got[which, q, pl.ds(pl.multiple_of(group * 16, 16), 16)].reshape(BLK, LANES)
            y = jnp.dot(perm[...], x, preferred_element_type=F32).astype(BF16)
            sorted_[:, pl.ds(pl.multiple_of(group * 64, 64), 64), :] = y.reshape(4, 64, LANES)
            return 0

        lax.fori_loop(0, 4, sort, 0)

        def use(n, _):
            block, mine = n // 2, 2 * half + n % 2
            lines = pl.ds(pl.multiple_of(mine * BLK, BLK), BLK)
            lanes = pl.ds(pl.multiple_of(d0 + block * LANES, LANES), LANES)
            y = sorted_[n]
            if which:
                acc[which, mine] += lax.dot_general(y, a[lines, lanes], NT, preferred_element_type=F32)
                a[lines, lanes] = jnp.dot(left_t[mine], y, preferred_element_type=F32).astype(BF16)
                pltpu.make_async_copy(a.at[lines, lanes], gv_hbm.at[lines, lanes], out_sem.at[0]).start()
            else:
                acc[which, mine] += lax.dot_general(dz[lines, lanes], y, NT, preferred_element_type=F32)
                z = jnp.dot(right[mine], y, preferred_element_type=F32)
                dy[lines, lanes] = (dy[lines, lanes].astype(F32) * z).astype(BF16)
                pltpu.make_async_copy(dy.at[lines, lanes], gg_hbm.at[lines, lanes], out_sem.at[1]).start()
            return 0

        lax.fori_loop(0, 4, use, 0)

    def exchange(which, half):
        return pltpu.make_async_remote_copy(
            src_ref=part.at[which, pl.ds(2 * half, 2)], dst_ref=part_in.at[which, pl.ds(2 * half, 2)],
            send_sem=cut_send.at[which, half], recv_sem=cut_recv.at[which, half],
            device_id=(other, me), device_id_type=MESH,
        )

    def hand_over(which, half):
        for block in (2 * half, 2 * half + 1):
            part[which, block] = acc[which, block].astype(BF16)
        exchange(which, half).start()

    def result(which, half):
        out = gl_hbm if which else gr_hbm
        here = pl.ds(2 * half, 2)
        return pltpu.make_async_copy(acc.at[which, here], out.at[here], out_sem.at[2 + 2 * which + half])

    def finish(which, half):
        exchange(which, half).wait_recv()
        for block in (2 * half, 2 * half + 1):
            acc[which, block] = part[which, block].astype(F32) + part_in[which, block].astype(F32)
        result(which, half).start()

    acc[...] = jnp.zeros_like(acc)
    o_block, o_half, o_dev, o_own = rows >> 7, (rows >> 6) & 1, (rows >> 2) & 15, rows & 3
    perm[...] = jnp.where(cols == 16 * o_dev + 8 * o_block + 2 * o_own + o_half, 1.0, 0.0).astype(BF16)

    loads[0].wait()
    build_expand(0)
    loads[1].wait()
    compute(0, 0)
    pl.semaphore_wait(barrier, N)
    send(0, 0)
    loads[2].wait()
    for q in (1, 2, 3):
        compute(0, q)
        send(0, q)

    loads[3].wait()
    build_expand(1)
    loads[4].wait()
    loads[5].wait()

    def gate(n, _):
        lines = pl.ds(pl.multiple_of(n * 16, 16), 16)
        dz[lines, :] = (dy[lines, :].astype(F32) * dz[lines, :].astype(F32)).astype(BF16)
        return 0

    lax.fori_loop(0, ROWS // 16, gate, 0)
    eye = jnp.where(rows == cols, 1.0, 0.0).astype(BF16)
    for block in range(OWN):
        left_t[block] = lax.dot_general(eye, left[block], NT, preferred_element_type=F32).astype(BF16)

    for q in range(4):
        compute(1, q)
        send(1, q)
        receive(0, q)
        if q % 2:
            hand_over(0, q // 2)
    for q in range(4):
        receive(1, q)
        if q % 2:
            hand_over(1, q // 2)
            finish(0, q // 2)
    finish(1, 0)
    finish(1, 1)

    pltpu.make_async_copy(a, gv_hbm, out_sem.at[0]).wait()
    pltpu.make_async_copy(dy, gg_hbm, out_sem.at[1]).wait()
    for which in range(2):
        for half in range(2):
            result(which, half).wait()
            exchange(which, half).wait_send()
        for q in range(4):
            all_of(which, q).wait_send()


def on_device(values_in, gate_out, grad_out, left_factor, right_factor):
    hbm = pl.BlockSpec(memory_space=pl.ANY)
    dma = pltpu.SemaphoreType.DMA
    grad_values, grad_gate, grad_left, grad_right = pl.pallas_call(
        kernel,
        name="mixer_backward",
        out_shape=(
            jax.ShapeDtypeStruct((ROWS, D), BF16),
            jax.ShapeDtypeStruct((ROWS, D), BF16),
            jax.ShapeDtypeStruct((OWN, BLK, BLK), F32),
            jax.ShapeDtypeStruct((OWN, BLK, BLK), F32),
        ),
        in_specs=[hbm] * 5,
        out_specs=(hbm,) * 4,
        scratch_shapes=[
            pltpu.VMEM((ROWS, D), BF16),
            pltpu.VMEM((ROWS, D), BF16),
            pltpu.VMEM((ROWS, D), BF16),
            pltpu.VMEM((OWN, BLK, BLK), BF16),
            pltpu.VMEM((OWN, BLK, BLK), BF16),
            pltpu.VMEM((OWN, BLK, BLK), BF16),
            pltpu.VMEM((2, 2, 2 * BLK, ROWS), BF16),
            pltpu.VMEM((BLK, BLK), BF16),
            pltpu.VMEM((2, 4, N, 16, LANES), BF16),
            pltpu.VMEM((2, 4, N, 16, LANES), BF16),
            pltpu.VMEM((4, BLK, LANES), BF16),
            pltpu.VMEM((2, OWN, BLK, BLK), F32),
            pltpu.VMEM((2, OWN, BLK, BLK), BF16),
            pltpu.VMEM((2, OWN, BLK, BLK), BF16),
            dma((6,)), dma((6,)), dma((2, 4)), dma((2, 4)), dma((2, 2)), dma((2, 2)),
        ],
        compiler_params=pltpu.CompilerParams(
            collective_id=0, has_side_effects=True, vmem_limit_bytes=56 * 1024 * 1024
        ),
        cost_estimate=pl.CostEstimate(flops=28 * ROWS * BLK * D, bytes_accessed=24 << 20, transcendentals=0),
    )(
        values_in.reshape(ROWS, D), gate_out.reshape(ROWS, D), grad_out.reshape(ROWS, D),
        left_factor, right_factor,
    )
    return grad_values.reshape(1, ROWS, D), grad_gate.reshape(1, ROWS, D), grad_left, grad_right


def solution(mesh):
    placed = P("cuts", "seq", None)
    factor = P("seq", None, None)
    return jax.shard_map(
        on_device,
        mesh=mesh,
        in_specs=(placed, placed, placed, factor, factor),
        out_specs=(placed, placed, factor, factor),
        check_vma=False,
    )
```

```python
import functools

import jax
import jax.numpy as jnp
from jax import lax
from jax.experimental import pallas as pl
from jax.experimental.pallas import tpu as pltpu
from jax.sharding import PartitionSpec as P

MESH = pl.DeviceIdType.MESH
F32 = jnp.float32
BF16 = jnp.bfloat16
N = 64
OWN = 4
BLK = 256
D = 2048
ROWS = OWN * BLK
LANES = 512
VMEM_LIMIT = 46 * 1024 * 1024
NT = (((1,), (1,)), ((), ()))


def peer(me, step):
    quarter, turn, z = step // 16, (step // 4) % 4, step % 4
    y = (z + turn) % 4
    pair = (quarter + z + 2 * turn + turn // 2) % 4
    core = me % 2
    z = (z + core * (4 - 2 * z)) % 4
    y = (y + core * (4 - 2 * y)) % 4
    to_z = (me // 16 + z) % 4
    to_x = (me // 8 + pair) % 2
    to_y = (me // 2 + y) % 4
    to_core = (core + pair // 2) % 2
    return ((to_z * 2 + to_x) * 4 + to_y) * 2 + to_core


def kernel(a_hbm, g_hbm, dy_hbm, l_hbm, r_hbm,
           a, dy, acc_left, acc_right,
           dz, left, right, left_t, expand, perm, sent, got, sorted_, part, part_in,
           in_sem, send_sem, recv_sem, cut_send, cut_recv):
    cut = lax.axis_index("cuts")
    me = lax.axis_index("seq")
    other = 1 - cut
    half_d = D // 2

    barrier = pltpu.get_barrier_semaphore()

    def greet(step, _):
        pl.semaphore_signal(barrier, inc=1, device_id=(cut, peer(me, step)), device_id_type=MESH)
        return 0

    lax.fori_loop(1, N, greet, 0)
    pl.semaphore_signal(barrier, inc=1, device_id=(other, me), device_id_type=MESH)

    lo, hi = pl.ds(0, half_d), pl.ds(half_d, half_d)
    loads = [
        pltpu.make_async_copy(l_hbm, left, in_sem.at[0]),
        pltpu.make_async_copy(a_hbm.at[:, lo], a.at[:, lo], in_sem.at[1]),
        pltpu.make_async_copy(a_hbm.at[:, hi], a.at[:, hi], in_sem.at[2]),
        pltpu.make_async_copy(r_hbm, right, in_sem.at[3]),
        pltpu.make_async_copy(dy_hbm, dy, in_sem.at[4]),
        pltpu.make_async_copy(g_hbm, dz, in_sem.at[5]),
    ]
    for load in loads:
        load.start()

    rows = lax.broadcasted_iota(jnp.int32, (BLK, BLK), 0)
    cols = lax.broadcasted_iota(jnp.int32, (BLK, BLK), 1)

    def build_expand(which):
        factor = right if which else left
        own = (rows >> 1) & 3

        def body(n, _):
            half, group = n // 2, n % 2
            hit = cols == 4 * (32 * group + (rows >> 3)) + 2 * half + (rows & 1)
            for block in range(OWN):
                pick = jnp.where(hit & (own == block), 1.0, 0.0).astype(BF16)
                if which:
                    out = lax.dot_general(pick, factor[block], NT, preferred_element_type=F32)
                else:
                    out = jnp.dot(pick, factor[block], preferred_element_type=F32)
                expand[which, half, pl.ds(pl.multiple_of(group * BLK, BLK), BLK), pl.ds(block * BLK, BLK)] = out.astype(BF16)
            return 0

        lax.fori_loop(0, 4, body, 0)

    def compute(which, q):
        half, d0 = q // 2, (q % 2) * half_d
        source = dz if which else a

        def body(n, _):
            group, tile = n // 2, n % 2
            take = pl.ds(pl.multiple_of(group * BLK, BLK), BLK)
            factor = expand[which, half, take, :]
            outs = []
            for block in range(2):
                lanes = pl.ds(pl.multiple_of(d0 + block * LANES + tile * 256, 256), 256)
                out = jnp.dot(factor, source[:, lanes], preferred_element_type=F32)
                outs.append(out.reshape(32, 8, 256))
            out = jnp.concatenate(outs, axis=1).astype(BF16)
            sent[which, q, pl.ds(pl.multiple_of(group * 32, 32), 32), :, pl.ds(pl.multiple_of(tile * 256, 256), 256)] = out
            return 0

        lax.fori_loop(0, 4, body, 0)
        got[which, q, me] = sent[which, q, me]

    def send(which, q):
        def body(step, _):
            to = peer(me, step)
            pltpu.make_async_remote_copy(
                src_ref=sent.at[which, q, to], dst_ref=got.at[which, q, me],
                send_sem=send_sem.at[which, q], recv_sem=recv_sem.at[which, q],
                device_id=(cut, to), device_id_type=MESH,
            ).start()
            return 0

        lax.fori_loop(1, N, body, 0)

    def all_of(which, q):
        span = pl.ds(0, N - 1)
        return pltpu.make_async_remote_copy(
            src_ref=sent.at[which, q, span], dst_ref=got.at[which, q, span],
            send_sem=send_sem.at[which, q], recv_sem=recv_sem.at[which, q],
            device_id=(cut, me), device_id_type=MESH,
        )

    def receive(which, q):
        half, d0 = q // 2, (q % 2) * half_d
        all_of(which, q).wait_recv()

        def sort(group, _):
            x = got[which, q, pl.ds(pl.multiple_of(group * 16, 16), 16)].reshape(BLK, LANES)
            y = jnp.dot(perm[...], x, preferred_element_type=F32).astype(BF16)
            sorted_[:, pl.ds(pl.multiple_of(group * 64, 64), 64), :] = y.reshape(4, 64, LANES)
            return 0

        lax.fori_loop(0, 4, sort, 0)

        def use(n, _):
            block, mine = n // 2, 2 * half + n % 2
            lines = pl.ds(pl.multiple_of(mine * BLK, BLK), BLK)
            lanes = pl.ds(pl.multiple_of(d0 + block * LANES, LANES), LANES)
            y = sorted_[n]
            if which:
                acc_left[mine] += lax.dot_general(y, a[lines, lanes], NT, preferred_element_type=F32)
                a[lines, lanes] = jnp.dot(left_t[mine], y, preferred_element_type=F32).astype(BF16)
            else:
                acc_right[mine] += lax.dot_general(dz[lines, lanes], y, NT, preferred_element_type=F32)
                z = jnp.dot(right[mine], y, preferred_element_type=F32)
                dy[lines, lanes] = (dy[lines, lanes].astype(F32) * z).astype(BF16)
            return 0

        lax.fori_loop(0, 4, use, 0)

    def exchange(which, half):
        return pltpu.make_async_remote_copy(
            src_ref=part.at[which, pl.ds(2 * half, 2)], dst_ref=part_in.at[which, pl.ds(2 * half, 2)],
            send_sem=cut_send.at[which, half], recv_sem=cut_recv.at[which, half],
            device_id=(other, me), device_id_type=MESH,
        )

    def hand_over(which, half):
        for block in (2 * half, 2 * half + 1):
            part[which, block] = (acc_left if which else acc_right)[block].astype(BF16)
        exchange(which, half).start()

    def finish(which, half):
        exchange(which, half).wait_recv()
        for block in (2 * half, 2 * half + 1):
            total = part[which, block].astype(F32) + part_in[which, block].astype(F32)
            if which:
                acc_left[block] = total
            else:
                acc_right[block] = total

    acc_left[...] = jnp.zeros_like(acc_left)
    acc_right[...] = jnp.zeros_like(acc_right)
    o_block, o_half, o_dev, o_own = rows >> 7, (rows >> 6) & 1, (rows >> 2) & 15, rows & 3
    perm[...] = jnp.where(cols == 16 * o_dev + 8 * o_block + 2 * o_own + o_half, 1.0, 0.0).astype(BF16)

    loads[0].wait()
    build_expand(0)
    loads[1].wait()
    compute(0, 0)
    pl.semaphore_wait(barrier, N)
    send(0, 0)
    loads[2].wait()
    for q in (1, 2, 3):
        compute(0, q)
        send(0, q)

    loads[3].wait()
    build_expand(1)
    loads[4].wait()
    loads[5].wait()

    def gate(n, _):
        lines = pl.ds(pl.multiple_of(n * 16, 16), 16)
        dz[lines, :] = (dy[lines, :].astype(F32) * dz[lines, :].astype(F32)).astype(BF16)
        return 0

    lax.fori_loop(0, ROWS // 16, gate, 0)
    eye = jnp.where(rows == cols, 1.0, 0.0).astype(BF16)
    for block in range(OWN):
        left_t[block] = lax.dot_general(eye, left[block], NT, preferred_element_type=F32).astype(BF16)

    for q in range(4):
        compute(1, q)
        send(1, q)
        receive(0, q)
        if q % 2:
            hand_over(0, q // 2)
    for q in range(4):
        receive(1, q)
        if q % 2:
            hand_over(1, q // 2)
            finish(0, q // 2)
    finish(1, 0)
    finish(1, 1)

    for which in range(2):
        for half in range(2):
            exchange(which, half).wait_send()
        for q in range(4):
            all_of(which, q).wait_send()


def write_out(gv, gg, gl, gr, gv_hbm, gg_hbm, gl_hbm, gr_hbm, sem):
    copies = []
    for n in range(OWN):
        lines = pl.ds(n * BLK, BLK)
        copies += [(gv.at[lines], gv_hbm.at[lines]), (gg.at[lines], gg_hbm.at[lines])]
        copies += [(gl.at[n], gl_hbm.at[n]), (gr.at[n], gr_hbm.at[n])]
    copies = [pltpu.make_async_copy(src, dst, sem.at[n]) for n, (src, dst) in enumerate(copies)]
    for copy in copies:
        copy.start()
    for copy in copies:
        copy.wait()


def on_device(values_in, gate_out, grad_out, left_factor, right_factor):
    hbm = pl.BlockSpec(memory_space=pl.ANY)
    vmem = pl.BlockSpec(memory_space=pltpu.VMEM)
    dma = pltpu.SemaphoreType.DMA
    shapes = (((ROWS, D), BF16), ((ROWS, D), BF16), ((OWN, BLK, BLK), F32), ((OWN, BLK, BLK), F32))
    held = pl.pallas_call(
        kernel,
        name="mixer_backward",
        out_shape=tuple(pltpu.VMEM(*shape) for shape in shapes),
        in_specs=[hbm] * 5,
        out_specs=(vmem,) * 4,
        scratch_shapes=[
            pltpu.VMEM((ROWS, D), BF16),
            pltpu.VMEM((OWN, BLK, BLK), BF16),
            pltpu.VMEM((OWN, BLK, BLK), BF16),
            pltpu.VMEM((OWN, BLK, BLK), BF16),
            pltpu.VMEM((2, 2, 2 * BLK, ROWS), BF16),
            pltpu.VMEM((BLK, BLK), BF16),
            pltpu.VMEM((2, 4, N, 16, LANES), BF16),
            pltpu.VMEM((2, 4, N, 16, LANES), BF16),
            pltpu.VMEM((4, BLK, LANES), BF16),
            pltpu.VMEM((2, OWN, BLK, BLK), BF16),
            pltpu.VMEM((2, OWN, BLK, BLK), BF16),
            dma((6,)), dma((2, 4)), dma((2, 4)), dma((2, 2)), dma((2, 2)),
        ],
        compiler_params=pltpu.CompilerParams(
            collective_id=0, has_side_effects=True, vmem_limit_bytes=VMEM_LIMIT
        ),
        cost_estimate=pl.CostEstimate(flops=28 * ROWS * BLK * D, bytes_accessed=14 << 20, transcendentals=0),
    )(
        values_in.reshape(ROWS, D), gate_out.reshape(ROWS, D), grad_out.reshape(ROWS, D),
        left_factor, right_factor,
    )
    grad_values, grad_gate, grad_left, grad_right = pl.pallas_call(
        write_out,
        name="write_out",
        out_shape=tuple(jax.ShapeDtypeStruct(*shape) for shape in shapes),
        in_specs=[hbm] * 4,
        out_specs=(hbm,) * 4,
        scratch_shapes=[dma((4 * OWN,))],
        compiler_params=pltpu.CompilerParams(vmem_limit_bytes=1 << 20),
        cost_estimate=pl.CostEstimate(flops=0, bytes_accessed=10 << 20, transcendentals=0),
    )(*held)
    return grad_values.reshape(1, ROWS, D), grad_gate.reshape(1, ROWS, D), grad_left, grad_right


def solution(mesh):
    placed = P("cuts", "seq", None)
    factor = P("seq", None, None)
    return jax.shard_map(
        on_device,
        mesh=mesh,
        in_specs=(placed, placed, placed, factor, factor),
        out_specs=(placed, placed, factor, factor),
        check_vma=False,
    )
```

```python
import functools

import jax
import jax.numpy as jnp
from jax import lax
from jax.experimental import pallas as pl
from jax.experimental.pallas import tpu as pltpu
from jax.sharding import PartitionSpec as P

MESH = pl.DeviceIdType.MESH
F32 = jnp.float32
BF16 = jnp.bfloat16
N = 64
OWN = 4
BLK = 256
D = 2048
ROWS = OWN * BLK
LANES = 512
VMEM_LIMIT = 46 * 1024 * 1024
NT = (((1,), (1,)), ((), ()))


def peer(me, far, step):
    turn, z = (step // 4) % 4, step % 4
    y = (z + turn) % 4
    core = me % 2
    flip = (step // 16 + z + turn) % 2
    to_z = (me // 16 + z + 2 * core) % 4
    to_x = (me // 8 + far) % 2
    to_y = (me // 2 + y + 2 * core) % 4
    to_core = (core + flip) % 2
    rest = to_y * 2 + to_core
    return to_z * 16 + to_x * 8 + rest, to_z * 8 + rest


def kernel(a_hbm, g_hbm, dy_hbm, l_hbm, r_hbm,
           a, dy, acc_left, acc_right,
           dz, left, right, left_t, expand, perm, sent, got, sorted_, part, part_in,
           in_sem, send_sem, recv_sem, cut_send, cut_recv):
    cut = lax.axis_index("cuts")
    me = lax.axis_index("seq")
    other = 1 - cut
    half_d = D // 2

    my_x = (me // 8) % 2
    lo, hi = pl.ds(0, half_d), pl.ds(half_d, half_d)
    loads = [
        pltpu.make_async_copy(l_hbm, left, in_sem.at[0]),
        pltpu.make_async_copy(a_hbm.at[:, lo], a.at[:, lo], in_sem.at[1]),
        pltpu.make_async_copy(a_hbm.at[:, hi], a.at[:, hi], in_sem.at[2]),
        pltpu.make_async_copy(r_hbm, right, in_sem.at[3]),
        pltpu.make_async_copy(dy_hbm, dy, in_sem.at[4]),
        pltpu.make_async_copy(g_hbm, dz, in_sem.at[5]),
    ]
    for load in loads:
        load.start()

    barrier = pltpu.get_barrier_semaphore()

    def greet(step, to):
        to = jnp.where(to == N - 1, 0, to + 1)
        pl.semaphore_signal(barrier, inc=1, device_id=(cut, to), device_id_type=MESH)
        return to

    lax.fori_loop(1, N, greet, me, unroll=9)
    pl.semaphore_signal(barrier, inc=1, device_id=(other, me), device_id_type=MESH)

    rows = lax.broadcasted_iota(jnp.int32, (BLK, BLK), 0)
    cols = lax.broadcasted_iota(jnp.int32, (BLK, BLK), 1)

    def build_expand(which, half, x):
        factor = right if which else left
        own = (rows >> 1) & 3
        to = rows >> 3
        hit = cols == 4 * (16 * (to >> 3) + 8 * x + (to & 7)) + 2 * half + (rows & 1)
        for block in range(OWN):
            pick = jnp.where(hit & (own == block), 1.0, 0.0).astype(BF16)
            if which:
                out = lax.dot_general(pick, factor[block], NT, preferred_element_type=F32)
            else:
                out = jnp.dot(pick, factor[block], preferred_element_type=F32)
            expand[which, half, x, :, pl.ds(block * BLK, BLK)] = out.astype(BF16)

    def build_rest(which, skip):
        def body(n, _):
            half, x = n // 2, (my_x + 1 + n) % 2
            build_expand(which, half, x)
            return 0

        lax.fori_loop(skip, 4, body, 0)

    def compute(which, q, x):
        half, d0 = q // 2, (q % 2) * half_d
        source = dz if which else a

        def body(tile, _):
            outs = []
            for block in range(2):
                lanes = pl.ds(pl.multiple_of(d0 + block * LANES + tile * 256, 256), 256)
                out = jnp.dot(expand[which, half, x], source[:, lanes], preferred_element_type=F32)
                outs.append(out.reshape(32, 8, 256))
            out = jnp.concatenate(outs, axis=1).astype(BF16)
            sent[which, q, x, :, :, pl.ds(pl.multiple_of(tile * 256, 256), 256)] = out
            return 0

        lax.fori_loop(0, LANES // 256, body, 0)

    def send(which, q, far):
        x = (my_x + far) % 2

        def body(step, _):
            to, place = peer(me, far, step)

            @pl.when(to != me)
            def _():
                pltpu.make_async_remote_copy(
                    src_ref=sent.at[which, q, x, place], dst_ref=got.at[which, q, me],
                    send_sem=send_sem.at[which, q], recv_sem=recv_sem.at[which, q],
                    device_id=(cut, to), device_id_type=MESH,
                ).start()

            return 0

        lax.fori_loop(0, N // 2, body, 0)

    def keep(which, q):
        got[which, q, me] = sent[which, q, my_x, (me // 16) * 8 + me % 8]

    def chunk(which, q):
        for far in (1, 0):
            compute(which, q, (my_x + far) % 2)
            send(which, q, far)
        keep(which, q)

    def all_of(which, q):
        span = pl.ds(0, N - 1)
        return pltpu.make_async_remote_copy(
            src_ref=got.at[which, q, span], dst_ref=got.at[which, q, span],
            send_sem=send_sem.at[which, q], recv_sem=recv_sem.at[which, q],
            device_id=(cut, me), device_id_type=MESH,
        )

    def receive(which, q):
        all_of(which, q).wait_recv()

        def sort(group, _):
            x = got[which, q, pl.ds(pl.multiple_of(group * 16, 16), 16)].reshape(BLK, LANES)
            y = jnp.dot(perm[...], x, preferred_element_type=F32).astype(BF16)
            sorted_[:, pl.ds(pl.multiple_of(group * 64, 64), 64), :] = y.reshape(4, 64, LANES)
            return 0

        lax.fori_loop(0, 4, sort, 0)

    def place_of(q, n):
        block, mine = n // 2, 2 * (q // 2) + n % 2
        lines = pl.ds(pl.multiple_of(mine * BLK, BLK), BLK)
        lanes = pl.ds(pl.multiple_of((q % 2) * half_d + block * LANES, LANES), LANES)
        return mine, lines, lanes

    def factor_gradient(which, q):
        def body(n, _):
            mine, lines, lanes = place_of(q, n)
            if which:
                acc_left[mine] += lax.dot_general(sorted_[n], a[lines, lanes], NT, preferred_element_type=F32)
            else:
                acc_right[mine] += lax.dot_general(dz[lines, lanes], sorted_[n], NT, preferred_element_type=F32)
            return 0

        lax.fori_loop(0, 4, body, 0)

    def row_gradient(which, q):
        def body(n, _):
            mine, lines, lanes = place_of(q, n)
            if which:
                a[lines, lanes] = jnp.dot(left_t[mine], sorted_[n], preferred_element_type=F32).astype(BF16)
            else:
                z = jnp.dot(right[mine], sorted_[n], preferred_element_type=F32)
                dy[lines, lanes] = (dy[lines, lanes].astype(F32) * z).astype(BF16)
            return 0

        lax.fori_loop(0, 4, body, 0)

    def exchange(which, half):
        return pltpu.make_async_remote_copy(
            src_ref=part.at[which, pl.ds(2 * half, 2)], dst_ref=part_in.at[which, pl.ds(2 * half, 2)],
            send_sem=cut_send.at[which, half], recv_sem=cut_recv.at[which, half],
            device_id=(other, me), device_id_type=MESH,
        )

    def hand_over(which, half):
        for block in (2 * half, 2 * half + 1):
            part[which, block] = (acc_left if which else acc_right)[block].astype(BF16)
        exchange(which, half).start()

    def finish(which, half):
        exchange(which, half).wait_recv()
        for block in (2 * half, 2 * half + 1):
            total = part[which, block].astype(F32) + part_in[which, block].astype(F32)
            if which:
                acc_left[block] = total
            else:
                acc_right[block] = total

    loads[0].wait()
    build_expand(0, 0, 1 - my_x)
    loads[1].wait()
    compute(0, 0, 1 - my_x)
    pl.semaphore_wait(barrier, N)
    send(0, 0, 1)
    build_expand(0, 0, my_x)
    compute(0, 0, my_x)
    send(0, 0, 0)
    keep(0, 0)
    loads[2].wait()
    chunk(0, 1)
    build_rest(0, 2)
    o_block, o_half, o_dev, o_own = rows >> 7, (rows >> 6) & 1, (rows >> 2) & 15, rows & 3
    perm[...] = jnp.where(cols == 16 * o_dev + 8 * o_block + 2 * o_own + o_half, 1.0, 0.0).astype(BF16)
    acc_left[...] = jnp.zeros_like(acc_left)
    acc_right[...] = jnp.zeros_like(acc_right)
    chunk(0, 2)
    chunk(0, 3)

    loads[3].wait()
    build_rest(1, 0)
    loads[4].wait()
    loads[5].wait()

    def gate(n, _):
        lines = pl.ds(pl.multiple_of(n * 16, 16), 16)
        dz[lines, :] = (dy[lines, :].astype(F32) * dz[lines, :].astype(F32)).astype(BF16)
        return 0

    lax.fori_loop(0, ROWS // 16, gate, 0)
    eye = jnp.where(rows == cols, 1.0, 0.0).astype(BF16)
    for block in range(OWN):
        left_t[block] = lax.dot_general(eye, left[block], NT, preferred_element_type=F32).astype(BF16)

    for q in range(4):
        chunk(1, q)
        receive(0, q)
        factor_gradient(0, q)
        if q % 2:
            hand_over(0, q // 2)
        row_gradient(0, q)
    for q in range(4):
        receive(1, q)
        factor_gradient(1, q)
        if q % 2:
            hand_over(1, q // 2)
        row_gradient(1, q)
        if q % 2:
            finish(0, q // 2)
    finish(1, 0)
    finish(1, 1)

    for which in range(2):
        for half in range(2):
            exchange(which, half).wait_send()
        for q in range(4):
            all_of(which, q).wait_send()


def write_out(gv, gg, gl, gr, gv_hbm, gg_hbm, gl_hbm, gr_hbm, sem):
    copies = []
    for n in range(OWN):
        lines = pl.ds(n * BLK, BLK)
        copies += [(gv.at[lines], gv_hbm.at[lines]), (gg.at[lines], gg_hbm.at[lines])]
        copies += [(gl.at[n], gl_hbm.at[n]), (gr.at[n], gr_hbm.at[n])]
    copies = [pltpu.make_async_copy(src, dst, sem.at[n]) for n, (src, dst) in enumerate(copies)]
    for copy in copies:
        copy.start()
    for copy in copies:
        copy.wait()


def on_device(values_in, gate_out, grad_out, left_factor, right_factor):
    hbm = pl.BlockSpec(memory_space=pl.ANY)
    vmem = pl.BlockSpec(memory_space=pltpu.VMEM)
    dma = pltpu.SemaphoreType.DMA
    shapes = (((ROWS, D), BF16), ((ROWS, D), BF16), ((OWN, BLK, BLK), F32), ((OWN, BLK, BLK), F32))
    held = pl.pallas_call(
        kernel,
        name="mixer_backward",
        out_shape=tuple(pltpu.VMEM(*shape) for shape in shapes),
        in_specs=[hbm] * 5,
        out_specs=(vmem,) * 4,
        scratch_shapes=[
            pltpu.VMEM((ROWS, D), BF16),
            pltpu.VMEM((OWN, BLK, BLK), BF16),
            pltpu.VMEM((OWN, BLK, BLK), BF16),
            pltpu.VMEM((OWN, BLK, BLK), BF16),
            pltpu.VMEM((2, 2, 2, BLK, ROWS), BF16),
            pltpu.VMEM((BLK, BLK), BF16),
            pltpu.VMEM((2, 4, 2, N // 2, 16, LANES), BF16),
            pltpu.VMEM((2, 4, N, 16, LANES), BF16),
            pltpu.VMEM((4, BLK, LANES), BF16),
            pltpu.VMEM((2, OWN, BLK, BLK), BF16),
            pltpu.VMEM((2, OWN, BLK, BLK), BF16),
            dma((6,)), dma((2, 4)), dma((2, 4)), dma((2, 2)), dma((2, 2)),
        ],
        compiler_params=pltpu.CompilerParams(
            collective_id=0, has_side_effects=True, vmem_limit_bytes=VMEM_LIMIT
        ),
        cost_estimate=pl.CostEstimate(flops=28 * ROWS * BLK * D, bytes_accessed=14 << 20, transcendentals=0),
    )(
        values_in.reshape(ROWS, D), gate_out.reshape(ROWS, D), grad_out.reshape(ROWS, D),
        left_factor, right_factor,
    )
    grad_values, grad_gate, grad_left, grad_right = pl.pallas_call(
        write_out,
        name="write_out",
        out_shape=tuple(jax.ShapeDtypeStruct(*shape) for shape in shapes),
        in_specs=[hbm] * 4,
        out_specs=(hbm,) * 4,
        scratch_shapes=[dma((4 * OWN,))],
        compiler_params=pltpu.CompilerParams(vmem_limit_bytes=1 << 20),
        cost_estimate=pl.CostEstimate(flops=0, bytes_accessed=10 << 20, transcendentals=0),
    )(*held)
    return grad_values.reshape(1, ROWS, D), grad_gate.reshape(1, ROWS, D), grad_left, grad_right


def solution(mesh):
    placed = P("cuts", "seq", None)
    factor = P("seq", None, None)
    return jax.shard_map(
        on_device,
        mesh=mesh,
        in_specs=(placed, placed, placed, factor, factor),
        out_specs=(placed, placed, factor, factor),
        check_vma=False,
    )
```

```python
import functools

import jax
import jax.numpy as jnp
from jax import lax
from jax.experimental import pallas as pl
from jax.experimental.pallas import tpu as pltpu
from jax.sharding import PartitionSpec as P

MESH = pl.DeviceIdType.MESH
F32 = jnp.float32
BF16 = jnp.bfloat16
N = 64
OWN = 4
BLK = 256
D = 2048
ROWS = OWN * BLK
LANES = 512
VMEM_LIMIT = 50 * 1024 * 1024
NT = (((1,), (1,)), ((), ()))


def peer(me, step):
    turn, z = (step // 4) % 4, step % 4
    y = (z + turn) % 4
    core = me % 2
    flip = (step // 16 + z + turn) % 2
    to_z = (me // 16 + z + 2 * core) % 4
    to_y = (me // 2 + y + 2 * core) % 4
    rest = to_y * 2 + (core + flip) % 2
    return to_z * 16 + (me // 8) % 2 * 8 + rest, to_z * 8 + rest


def kernel(a_hbm, g_hbm, dy_hbm, l_hbm, r_hbm,
           a, dy, acc_left, acc_right,
           dz, left, right, left_t, expand, perm, sent, relay, got, sorted_, part, part_in,
           in_sem, send_sem, recv_sem, x_send, x_recv, cut_send, cut_recv, pair_in, rows_in, cut_in, all_in):
    cut = lax.axis_index("cuts")
    me = lax.axis_index("seq")
    other = 1 - cut
    half_d = D // 2

    my_x = (me // 8) % 2
    lo, hi = pl.ds(0, half_d), pl.ds(half_d, half_d)
    loads = [
        pltpu.make_async_copy(l_hbm, left, in_sem.at[0]),
        pltpu.make_async_copy(a_hbm.at[:, lo], a.at[:, lo], in_sem.at[1]),
        pltpu.make_async_copy(a_hbm.at[:, hi], a.at[:, hi], in_sem.at[2]),
        pltpu.make_async_copy(r_hbm, right, in_sem.at[3]),
        pltpu.make_async_copy(dy_hbm, dy, in_sem.at[4]),
        pltpu.make_async_copy(g_hbm, dz, in_sem.at[5]),
    ]
    for load in loads[:2]:
        load.start()

    near_side, lead = my_x == 0, me == 0
    partner = me + 8 - 16 * my_x
    my_place = (me // 16) * 8 + me % 8

    def tell(semaphore, to_cut, to):
        pl.semaphore_signal(semaphore, inc=1, device_id=(to_cut, to), device_id_type=MESH)

    def tell_rows(semaphore):
        def body(n, _):
            tell(semaphore, cut, (n // 8) * 16 + n % 8)
            return 0

        lax.fori_loop(1, N // 2, body, 0)

    barrier = pltpu.get_barrier_semaphore()

    @pl.when(near_side)
    def _():
        tell(barrier, cut, partner)

    @pl.when(lead)
    def _():
        tell(barrier, other, 0)
        tell_rows(barrier)

    def meet_partner():
        pl.semaphore_wait(barrier, 1)

        @pl.when(near_side)
        def _():
            pl.semaphore_wait(pair_in, 1)

            @pl.when(me != 0)
            def _():
                tell(rows_in, cut, 0)

        @pl.when(my_x == 1)
        def _():
            tell(pair_in, cut, partner)

    def meet_all():
        @pl.when(lead)
        def _():
            pl.semaphore_wait(rows_in, N // 2 - 1)
            tell(cut_in, other, 0)
            pl.semaphore_wait(cut_in, 1)
            tell_rows(all_in)

        @pl.when(me != 0)
        def _():
            pl.semaphore_wait(all_in, 1)

        @pl.when(near_side)
        def _():
            tell(all_in, cut, partner)

    rows = lax.broadcasted_iota(jnp.int32, (BLK, BLK), 0)
    cols = lax.broadcasted_iota(jnp.int32, (BLK, BLK), 1)

    def build_expand(which, half, x):
        factor = right if which else left
        own = (rows >> 1) & 3
        to = rows >> 3
        hit = cols == 4 * (16 * (to >> 3) + 8 * x + (to & 7)) + 2 * half + (rows & 1)
        for block in range(OWN):
            pick = jnp.where(hit & (own == block), 1.0, 0.0).astype(BF16)
            if which:
                out = lax.dot_general(pick, factor[block], NT, preferred_element_type=F32)
            else:
                out = jnp.dot(pick, factor[block], preferred_element_type=F32)
            expand[which, half, x, :, pl.ds(block * BLK, BLK)] = out.astype(BF16)

    def build_rest(which, skip):
        def body(n, _):
            half, x = n // 2, (my_x + 1 + n) % 2
            build_expand(which, half, x)
            return 0

        lax.fori_loop(skip, 4, body, 0)

    def compute(which, q, x):
        half, d0 = q // 2, (q % 2) * half_d
        source = dz if which else a

        def body(tile, _):
            outs = []
            for block in range(2):
                lanes = pl.ds(pl.multiple_of(d0 + block * LANES + tile * 256, 256), 256)
                out = jnp.dot(expand[which, half, x], source[:, lanes], preferred_element_type=F32)
                outs.append(out.reshape(32, 8, 256))
            out = jnp.concatenate(outs, axis=1).astype(BF16)
            sent[which, q, x, :, :, pl.ds(pl.multiple_of(tile * 256, 256), 256)] = out
            return 0

        lax.fori_loop(0, LANES // 256, body, 0)

    def to_peers(which, q, source, origin):
        def body(step, _):
            to, place = peer(me, step)

            @pl.when(to != me)
            def _():
                pltpu.make_async_remote_copy(
                    src_ref=source.at[place], dst_ref=got.at[which, q, origin],
                    send_sem=send_sem.at[which, q], recv_sem=recv_sem.at[which, q],
                    device_id=(cut, to), device_id_type=MESH,
                ).start()

            return 0

        lax.fori_loop(0, N // 2, body, 0)

    def across(which, q):
        return pltpu.make_async_remote_copy(
            src_ref=sent.at[which, q, 1 - my_x], dst_ref=relay.at[which, q],
            send_sem=x_send.at[which, q], recv_sem=x_recv.at[which, q],
            device_id=(cut, partner), device_id_type=MESH,
        )

    def send_near(which, q):
        to_peers(which, q, sent.at[which, q, my_x], me)
        got[which, q, me] = sent[which, q, my_x, my_place]

    def forward(which, q):
        across(which, q).wait_recv()
        to_peers(which, q, relay.at[which, q], partner)
        got[which, q, partner] = relay[which, q, my_place]

    def chunk(which, q):
        compute(which, q, 1 - my_x)
        across(which, q).start()
        compute(which, q, my_x)

    def all_of(which, q):
        span = pl.ds(0, N - 2)
        return pltpu.make_async_remote_copy(
            src_ref=got.at[which, q, span], dst_ref=got.at[which, q, span],
            send_sem=send_sem.at[which, q], recv_sem=recv_sem.at[which, q],
            device_id=(cut, me), device_id_type=MESH,
        )

    def receive(which, q):
        all_of(which, q).wait_recv()

        def sort(group, _):
            x = got[which, q, pl.ds(pl.multiple_of(group * 16, 16), 16)].reshape(BLK, LANES)
            y = jnp.dot(perm[...], x, preferred_element_type=F32).astype(BF16)
            sorted_[:, pl.ds(pl.multiple_of(group * 64, 64), 64), :] = y.reshape(4, 64, LANES)
            return 0

        lax.fori_loop(0, 4, sort, 0)

    def place_of(q, n):
        block, mine = n // 2, 2 * (q // 2) + n % 2
        lines = pl.ds(pl.multiple_of(mine * BLK, BLK), BLK)
        lanes = pl.ds(pl.multiple_of((q % 2) * half_d + block * LANES, LANES), LANES)
        return mine, lines, lanes

    def factor_gradient(which, q):
        def body(n, _):
            mine, lines, lanes = place_of(q, n)
            if which:
                acc_left[mine] += lax.dot_general(sorted_[n], a[lines, lanes], NT, preferred_element_type=F32)
            else:
                acc_right[mine] += lax.dot_general(dz[lines, lanes], sorted_[n], NT, preferred_element_type=F32)
            return 0

        lax.fori_loop(0, 4, body, 0)

    def row_gradient(which, q):
        def body(n, _):
            mine, lines, lanes = place_of(q, n)
            if which:
                a[lines, lanes] = jnp.dot(left_t[mine], sorted_[n], preferred_element_type=F32).astype(BF16)
            else:
                z = jnp.dot(right[mine], sorted_[n], preferred_element_type=F32)
                dy[lines, lanes] = (dy[lines, lanes].astype(F32) * z).astype(BF16)
            return 0

        lax.fori_loop(0, 4, body, 0)

    def exchange(which, half):
        return pltpu.make_async_remote_copy(
            src_ref=part.at[which, pl.ds(2 * half, 2)], dst_ref=part_in.at[which, pl.ds(2 * half, 2)],
            send_sem=cut_send.at[which, half], recv_sem=cut_recv.at[which, half],
            device_id=(other, me), device_id_type=MESH,
        )

    def hand_over(which, half):
        for block in (2 * half, 2 * half + 1):
            part[which, block] = (acc_left if which else acc_right)[block].astype(BF16)

    def finish(which, half):
        exchange(which, half).wait_recv()
        for block in (2 * half, 2 * half + 1):
            total = part[which, block].astype(F32) + part_in[which, block].astype(F32)
            if which:
                acc_left[block] = total
            else:
                acc_right[block] = total

    loads[0].wait()
    build_expand(0, 0, 1 - my_x)
    loads[1].wait()
    for load in loads[2:]:
        load.start()
    compute(0, 0, 1 - my_x)
    meet_partner()
    across(0, 0).start()
    build_expand(0, 0, my_x)
    compute(0, 0, my_x)
    loads[2].wait()
    chunk(0, 1)
    meet_all()
    send_near(0, 0)
    send_near(0, 1)
    build_rest(0, 2)
    o_block, o_half, o_dev, o_own = rows >> 7, (rows >> 6) & 1, (rows >> 2) & 15, rows & 3
    perm[...] = jnp.where(cols == 16 * o_dev + 8 * o_block + 2 * o_own + o_half, 1.0, 0.0).astype(BF16)
    acc_left[...] = jnp.zeros_like(acc_left)
    acc_right[...] = jnp.zeros_like(acc_right)
    for q in (2, 3):
        chunk(0, q)
        send_near(0, q)

    loads[3].wait()
    build_rest(1, 0)
    loads[4].wait()
    loads[5].wait()

    def gate(n, _):
        lines = pl.ds(pl.multiple_of(n * 16, 16), 16)
        dz[lines, :] = (dy[lines, :].astype(F32) * dz[lines, :].astype(F32)).astype(BF16)
        return 0

    lax.fori_loop(0, ROWS // 16, gate, 0)
    eye = jnp.where(rows == cols, 1.0, 0.0).astype(BF16)
    for block in range(OWN):
        left_t[block] = lax.dot_general(eye, left[block], NT, preferred_element_type=F32).astype(BF16)

    def work(n):
        which, q = n // 4, n % 4
        receive(which, q)
        factor_gradient(which, q)
        if q % 2:
            hand_over(which, q // 2)
        row_gradient(which, q)

    for q in range(4):
        chunk(1, q)
        send_near(1, q)
        if q == 1:
            forward(0, 0)
    forward(0, 1)
    for n in range(2, 8):
        forward(n // 4, n % 4)
        if n == 7:
            exchange(0, 0).start()
            exchange(0, 1).start()
        work(n - 2)
    exchange(1, 0).start()
    work(6)
    receive(1, 3)
    factor_gradient(1, 3)
    hand_over(1, 1)
    exchange(1, 1).start()
    row_gradient(1, 3)
    for n in range(4):
        finish(n // 2, n % 2)

    for which in range(2):
        for half in range(2):
            exchange(which, half).wait_send()
        for q in range(4):
            all_of(which, q).wait_send()
            across(which, q).wait_send()


def write_out(gv, gg, gl, gr, gv_hbm, gg_hbm, gl_hbm, gr_hbm, sem):
    copies = []
    for n in range(OWN):
        lines = pl.ds(n * BLK, BLK)
        copies += [(gv.at[lines], gv_hbm.at[lines]), (gg.at[lines], gg_hbm.at[lines])]
        copies += [(gl.at[n], gl_hbm.at[n]), (gr.at[n], gr_hbm.at[n])]
    copies = [pltpu.make_async_copy(src, dst, sem.at[n]) for n, (src, dst) in enumerate(copies)]
    for copy in copies:
        copy.start()
    for copy in copies:
        copy.wait()


def on_device(values_in, gate_out, grad_out, left_factor, right_factor):
    hbm = pl.BlockSpec(memory_space=pl.ANY)
    vmem = pl.BlockSpec(memory_space=pltpu.VMEM)
    dma = pltpu.SemaphoreType.DMA
    shapes = (((ROWS, D), BF16), ((ROWS, D), BF16), ((OWN, BLK, BLK), F32), ((OWN, BLK, BLK), F32))
    held = pl.pallas_call(
        kernel,
        name="mixer_backward",
        out_shape=tuple(pltpu.VMEM(*shape) for shape in shapes),
        in_specs=[hbm] * 5,
        out_specs=(vmem,) * 4,
        scratch_shapes=[
            pltpu.VMEM((ROWS, D), BF16),
            pltpu.VMEM((OWN, BLK, BLK), BF16),
            pltpu.VMEM((OWN, BLK, BLK), BF16),
            pltpu.VMEM((OWN, BLK, BLK), BF16),
            pltpu.VMEM((2, 2, 2, BLK, ROWS), BF16),
            pltpu.VMEM((BLK, BLK), BF16),
            pltpu.VMEM((2, 4, 2, N // 2, 16, LANES), BF16),
            pltpu.VMEM((2, 4, N // 2, 16, LANES), BF16),
            pltpu.VMEM((2, 4, N, 16, LANES), BF16),
            pltpu.VMEM((4, BLK, LANES), BF16),
            pltpu.VMEM((2, OWN, BLK, BLK), BF16),
            pltpu.VMEM((2, OWN, BLK, BLK), BF16),
            dma((6,)), dma((2, 4)), dma((2, 4)), dma((2, 4)), dma((2, 4)), dma((2, 2)), dma((2, 2)),
            *[pltpu.SemaphoreType.REGULAR] * 4,
        ],
        compiler_params=pltpu.CompilerParams(
            collective_id=0, has_side_effects=True, vmem_limit_bytes=VMEM_LIMIT
        ),
        cost_estimate=pl.CostEstimate(flops=28 * ROWS * BLK * D, bytes_accessed=14 << 20, transcendentals=0),
    )(
        values_in.reshape(ROWS, D), gate_out.reshape(ROWS, D), grad_out.reshape(ROWS, D),
        left_factor, right_factor,
    )
    grad_values, grad_gate, grad_left, grad_right = pl.pallas_call(
        write_out,
        name="write_out",
        out_shape=tuple(jax.ShapeDtypeStruct(*shape) for shape in shapes),
        in_specs=[hbm] * 4,
        out_specs=(hbm,) * 4,
        scratch_shapes=[dma((4 * OWN,))],
        compiler_params=pltpu.CompilerParams(vmem_limit_bytes=1 << 20),
        cost_estimate=pl.CostEstimate(flops=0, bytes_accessed=10 << 20, transcendentals=0),
    )(*held)
    return grad_values.reshape(1, ROWS, D), grad_gate.reshape(1, ROWS, D), grad_left, grad_right


def solution(mesh):
    placed = P("cuts", "seq", None)
    factor = P("seq", None, None)
    return jax.shard_map(
        on_device,
        mesh=mesh,
        in_specs=(placed, placed, placed, factor, factor),
        out_specs=(placed, placed, factor, factor),
        check_vma=False,
    )
```

```python
import functools

import jax
import jax.numpy as jnp
from jax import lax
from jax.experimental import pallas as pl
from jax.experimental.pallas import tpu as pltpu
from jax.sharding import PartitionSpec as P

MESH = pl.DeviceIdType.MESH
F32 = jnp.float32
BF16 = jnp.bfloat16
N = 64
OWN = 4
BLK = 256
D = 2048
ROWS = OWN * BLK
LANES = 512
VMEM_LIMIT = 50 * 1024 * 1024
NT = (((1,), (1,)), ((), ()))


def peer(me, step):
    turn, z = (step // 4) % 4, step % 4
    y = (z + turn) % 4
    core = me % 2
    flip = (step // 16 + z + turn) % 2
    to_z = (me // 16 + z + 2 * core) % 4
    to_y = (me // 2 + y + 2 * core) % 4
    rest = to_y * 2 + (core + flip) % 2
    return to_z * 16 + (me // 8) % 2 * 8 + rest, to_z * 8 + rest


def kernel(a_hbm, g_hbm, dy_hbm, l_hbm, r_hbm,
           a, dy, acc_left, acc_right,
           dz, left, right, left_t, expand, perm, sent, relay, got, sorted_, part, part_in,
           in_sem, send_sem, recv_sem, x_send, x_recv, cut_send, cut_recv, pair_in, rows_in, cut_in, all_in):
    cut = lax.axis_index("cuts")
    me = lax.axis_index("seq")
    other = 1 - cut
    half_d = D // 2

    my_x = (me // 8) % 2
    def tile_load(n):
        lanes = pl.ds(n * 256, 256)
        return pltpu.make_async_copy(a_hbm.at[:, lanes], a.at[:, lanes], in_sem.at[n])

    left_load = pltpu.make_async_copy(l_hbm, left, in_sem.at[4])
    tile_loads = [tile_load(n) for n in (0, 2, 1, 3)]
    hi = pl.ds(half_d, half_d)
    a_load = pltpu.make_async_copy(a_hbm.at[:, hi], a.at[:, hi], in_sem.at[5])
    other_loads = [
        pltpu.make_async_copy(r_hbm, right, in_sem.at[6]),
        pltpu.make_async_copy(dy_hbm, dy, in_sem.at[7]),
        pltpu.make_async_copy(g_hbm, dz, in_sem.at[8]),
    ]
    left_load.start()
    for load in tile_loads:
        load.start()

    near_side, lead = my_x == 0, me == 0
    partner = me + 8 - 16 * my_x
    my_place = (me // 16) * 8 + me % 8

    def tell(semaphore, to_cut, to):
        pl.semaphore_signal(semaphore, inc=1, device_id=(to_cut, to), device_id_type=MESH)

    def tell_rows(semaphore):
        def body(n, _):
            tell(semaphore, cut, (n // 8) * 16 + n % 8)
            return 0

        lax.fori_loop(1, N // 2, body, 0)

    barrier = pltpu.get_barrier_semaphore()

    @pl.when(near_side)
    def _():
        tell(barrier, cut, partner)

    @pl.when(lead)
    def _():
        tell(barrier, other, 0)
        tell_rows(barrier)

    @pl.when(my_x == 1)
    def _():
        pl.semaphore_wait(barrier, 1)
        tell(pair_in, cut, partner)

    def meet_partner():
        @pl.when(near_side)
        def _():
            pl.semaphore_wait(barrier, 1)
            pl.semaphore_wait(pair_in, 1)

            @pl.when(me != 0)
            def _():
                tell(rows_in, cut, 0)

    def meet_cut():
        @pl.when(lead)
        def _():
            pl.semaphore_wait(rows_in, N // 2 - 1)
            tell_rows(all_in)
            tell(cut_in, other, 0)

        @pl.when(me != 0)
        def _():
            pl.semaphore_wait(all_in, 1)

        @pl.when(near_side)
        def _():
            tell(all_in, cut, partner)

    def meet_other_cut():
        @pl.when(lead)
        def _():
            pl.semaphore_wait(cut_in, 1)
            tell_rows(all_in)

        @pl.when(me != 0)
        def _():
            pl.semaphore_wait(all_in, 1)

        @pl.when(near_side)
        def _():
            tell(all_in, cut, partner)

    rows = lax.broadcasted_iota(jnp.int32, (BLK, BLK), 0)
    cols = lax.broadcasted_iota(jnp.int32, (BLK, BLK), 1)

    def build_expand(which, half, x):
        factor = right if which else left
        own = (rows >> 1) & 3
        to = rows >> 3
        hit = cols == 4 * (16 * (to >> 3) + 8 * x + (to & 7)) + 2 * half + (rows & 1)
        for block in range(OWN):
            pick = jnp.where(hit & (own == block), 1.0, 0.0).astype(BF16)
            if which:
                out = lax.dot_general(pick, factor[block], NT, preferred_element_type=F32)
            else:
                out = jnp.dot(pick, factor[block], preferred_element_type=F32)
            expand[which, half, x, :, pl.ds(block * BLK, BLK)] = out.astype(BF16)

    def build_rest(which, skip):
        def body(n, _):
            half, x = n // 2, (my_x + 1 + n) % 2
            build_expand(which, half, x)
            return 0

        lax.fori_loop(skip, 4, body, 0)

    def compute_tile(which, q, x, tile):
        half, d0 = q // 2, (q % 2) * half_d
        source = dz if which else a
        outs = []
        for block in range(2):
            lanes = pl.ds(pl.multiple_of(d0 + block * LANES + tile * 256, 256), 256)
            out = jnp.dot(expand[which, half, x], source[:, lanes], preferred_element_type=F32)
            outs.append(out.reshape(32, 8, 256))
        out = jnp.concatenate(outs, axis=1).astype(BF16)
        sent[which, q, x, :, :, pl.ds(pl.multiple_of(tile * 256, 256), 256)] = out

    def compute(which, q, x):
        def body(tile, _):
            compute_tile(which, q, x, tile)
            return 0

        lax.fori_loop(0, LANES // 256, body, 0)

    def to_peers(which, q, source, origin):
        def body(step, _):
            to, place = peer(me, step)

            @pl.when(to != me)
            def _():
                pltpu.make_async_remote_copy(
                    src_ref=source.at[place], dst_ref=got.at[which, q, origin],
                    send_sem=send_sem.at[which, q], recv_sem=recv_sem.at[which, q],
                    device_id=(cut, to), device_id_type=MESH,
                ).start()

            return 0

        lax.fori_loop(0, N // 2, body, 0)

    def across(which, q, lanes=pl.ds(0, LANES)):
        return pltpu.make_async_remote_copy(
            src_ref=sent.at[which, q, 1 - my_x, :, :, lanes], dst_ref=relay.at[which, q, :, :, lanes],
            send_sem=x_send.at[which, q], recv_sem=x_recv.at[which, q],
            device_id=(cut, partner), device_id_type=MESH,
        )

    def send_near(which, q):
        to_peers(which, q, sent.at[which, q, my_x], me)
        got[which, q, me] = sent[which, q, my_x, my_place]

    def forward(which, q):
        to_peers(which, q, relay.at[which, q], partner)
        got[which, q, partner] = relay[which, q, my_place]

    def chunk(which, q):
        compute(which, q, 1 - my_x)
        across(which, q).start()
        compute(which, q, my_x)

    def all_of(which, q):
        span = pl.ds(0, N - 2)
        return pltpu.make_async_remote_copy(
            src_ref=got.at[which, q, span], dst_ref=got.at[which, q, span],
            send_sem=send_sem.at[which, q], recv_sem=recv_sem.at[which, q],
            device_id=(cut, me), device_id_type=MESH,
        )

    def receive(which, q):
        all_of(which, q).wait_recv()

        def sort(group, _):
            x = got[which, q, pl.ds(pl.multiple_of(group * 16, 16), 16)].reshape(BLK, LANES)
            y = jnp.dot(perm[...], x, preferred_element_type=F32).astype(BF16)
            sorted_[:, pl.ds(pl.multiple_of(group * 64, 64), 64), :] = y.reshape(4, 64, LANES)
            return 0

        lax.fori_loop(0, 4, sort, 0)

    def place_of(q, n):
        block, mine = n // 2, 2 * (q // 2) + n % 2
        lines = pl.ds(pl.multiple_of(mine * BLK, BLK), BLK)
        lanes = pl.ds(pl.multiple_of((q % 2) * half_d + block * LANES, LANES), LANES)
        return mine, lines, lanes

    def factor_gradient(which, q):
        def body(n, _):
            mine, lines, lanes = place_of(q, n)
            if which:
                acc_left[mine] += lax.dot_general(sorted_[n], a[lines, lanes], NT, preferred_element_type=F32)
            else:
                acc_right[mine] += lax.dot_general(dz[lines, lanes], sorted_[n], NT, preferred_element_type=F32)
            return 0

        lax.fori_loop(0, 4, body, 0)

    def row_gradient(which, q):
        def body(n, _):
            mine, lines, lanes = place_of(q, n)
            if which:
                a[lines, lanes] = jnp.dot(left_t[mine], sorted_[n], preferred_element_type=F32).astype(BF16)
            else:
                z = jnp.dot(right[mine], sorted_[n], preferred_element_type=F32)
                dy[lines, lanes] = (dy[lines, lanes].astype(F32) * z).astype(BF16)
            return 0

        lax.fori_loop(0, 4, body, 0)

    def exchange(which, half):
        return pltpu.make_async_remote_copy(
            src_ref=part.at[which, pl.ds(2 * half, 2)], dst_ref=part_in.at[which, pl.ds(2 * half, 2)],
            send_sem=cut_send.at[which, half], recv_sem=cut_recv.at[which, half],
            device_id=(other, me), device_id_type=MESH,
        )

    def hand_over(which, half):
        for block in (2 * half, 2 * half + 1):
            part[which, block] = (acc_left if which else acc_right)[block].astype(BF16)

    def finish(which, half):
        exchange(which, half).wait_recv()
        for block in (2 * half, 2 * half + 1):
            total = part[which, block].astype(F32) + part_in[which, block].astype(F32)
            if which:
                acc_left[block] = total
            else:
                acc_right[block] = total

    left_load.wait()
    build_expand(0, 0, 1 - my_x)
    meet_partner()
    for tile in range(2):
        tile_loads[2 * tile].wait()
        tile_loads[2 * tile + 1].wait()
        if tile == 1:
            a_load.start()
        compute_tile(0, 0, 1 - my_x, tile)
        across(0, 0, pl.ds(tile * 256, 256)).start()
    for load in other_loads:
        load.start()
    build_expand(0, 0, my_x)
    compute(0, 0, my_x)
    meet_cut()
    send_near(0, 0)
    a_load.wait()
    chunk(0, 1)
    send_near(0, 1)
    build_rest(0, 2)
    o_block, o_half, o_dev, o_own = rows >> 7, (rows >> 6) & 1, (rows >> 2) & 15, rows & 3
    perm[...] = jnp.where(cols == 16 * o_dev + 8 * o_block + 2 * o_own + o_half, 1.0, 0.0).astype(BF16)
    acc_left[...] = jnp.zeros_like(acc_left)
    acc_right[...] = jnp.zeros_like(acc_right)
    for q in (2, 3):
        chunk(0, q)
        send_near(0, q)

    other_loads[0].wait()
    build_rest(1, 0)
    other_loads[1].wait()
    other_loads[2].wait()

    def gate(n, _):
        lines = pl.ds(pl.multiple_of(n * 16, 16), 16)
        dz[lines, :] = (dy[lines, :].astype(F32) * dz[lines, :].astype(F32)).astype(BF16)
        return 0

    lax.fori_loop(0, ROWS // 16, gate, 0)
    eye = jnp.where(rows == cols, 1.0, 0.0).astype(BF16)
    for block in range(OWN):
        left_t[block] = lax.dot_general(eye, left[block], NT, preferred_element_type=F32).astype(BF16)

    def work(n):
        which, q = n // 4, n % 4
        receive(which, q)
        factor_gradient(which, q)
        if q % 2:
            hand_over(which, q // 2)
        row_gradient(which, q)

    for q in range(4):
        chunk(1, q)
        send_near(1, q)
        if q == 1:
            across(0, 0).wait_recv()
            forward(0, 0)
    meet_other_cut()
    across(0, 1).wait_recv()
    forward(0, 1)
    for n in range(2, 8):
        across(n // 4, n % 4).wait_recv()
        if n == 6:
            exchange(0, 0).start()
        if n == 7:
            exchange(0, 1).start()
        forward(n // 4, n % 4)
        work(n - 2)
    exchange(1, 0).start()
    work(6)
    receive(1, 3)
    factor_gradient(1, 3)
    hand_over(1, 1)
    exchange(1, 1).start()
    row_gradient(1, 3)
    for n in range(4):
        finish(n // 2, n % 2)

    for which in range(2):
        for half in range(2):
            exchange(which, half).wait_send()
        for q in range(4):
            all_of(which, q).wait_send()
            across(which, q).wait_send()


def write_out(gv, gg, gl, gr, gv_hbm, gg_hbm, gl_hbm, gr_hbm, sem):
    copies = []
    for n in range(OWN):
        lines = pl.ds(n * BLK, BLK)
        copies += [(gv.at[lines], gv_hbm.at[lines]), (gg.at[lines], gg_hbm.at[lines])]
        copies += [(gl.at[n], gl_hbm.at[n]), (gr.at[n], gr_hbm.at[n])]
    copies = [pltpu.make_async_copy(src, dst, sem.at[n]) for n, (src, dst) in enumerate(copies)]
    for copy in copies:
        copy.start()
    for copy in copies:
        copy.wait()


def on_device(values_in, gate_out, grad_out, left_factor, right_factor):
    hbm = pl.BlockSpec(memory_space=pl.ANY)
    vmem = pl.BlockSpec(memory_space=pltpu.VMEM)
    dma = pltpu.SemaphoreType.DMA
    shapes = (((ROWS, D), BF16), ((ROWS, D), BF16), ((OWN, BLK, BLK), F32), ((OWN, BLK, BLK), F32))
    held = pl.pallas_call(
        kernel,
        name="mixer_backward",
        out_shape=tuple(pltpu.VMEM(*shape) for shape in shapes),
        in_specs=[hbm] * 5,
        out_specs=(vmem,) * 4,
        scratch_shapes=[
            pltpu.VMEM((ROWS, D), BF16),
            pltpu.VMEM((OWN, BLK, BLK), BF16),
            pltpu.VMEM((OWN, BLK, BLK), BF16),
            pltpu.VMEM((OWN, BLK, BLK), BF16),
            pltpu.VMEM((2, 2, 2, BLK, ROWS), BF16),
            pltpu.VMEM((BLK, BLK), BF16),
            pltpu.VMEM((2, 4, 2, N // 2, 16, LANES), BF16),
            pltpu.VMEM((2, 4, N // 2, 16, LANES), BF16),
            pltpu.VMEM((2, 4, N, 16, LANES), BF16),
            pltpu.VMEM((4, BLK, LANES), BF16),
            pltpu.VMEM((2, OWN, BLK, BLK), BF16),
            pltpu.VMEM((2, OWN, BLK, BLK), BF16),
            dma((9,)), dma((2, 4)), dma((2, 4)), dma((2, 4)), dma((2, 4)), dma((2, 2)), dma((2, 2)),
            *[pltpu.SemaphoreType.REGULAR] * 4,
        ],
        compiler_params=pltpu.CompilerParams(
            collective_id=0, has_side_effects=True, vmem_limit_bytes=VMEM_LIMIT
        ),
        cost_estimate=pl.CostEstimate(flops=28 * ROWS * BLK * D, bytes_accessed=14 << 20, transcendentals=0),
    )(
        values_in.reshape(ROWS, D), gate_out.reshape(ROWS, D), grad_out.reshape(ROWS, D),
        left_factor, right_factor,
    )
    grad_values, grad_gate, grad_left, grad_right = pl.pallas_call(
        write_out,
        name="write_out",
        out_shape=tuple(jax.ShapeDtypeStruct(*shape) for shape in shapes),
        in_specs=[hbm] * 4,
        out_specs=(hbm,) * 4,
        scratch_shapes=[dma((4 * OWN,))],
        compiler_params=pltpu.CompilerParams(vmem_limit_bytes=1 << 20),
        cost_estimate=pl.CostEstimate(flops=0, bytes_accessed=10 << 20, transcendentals=0),
    )(*held)
    return grad_values.reshape(1, ROWS, D), grad_gate.reshape(1, ROWS, D), grad_left, grad_right


def solution(mesh):
    placed = P("cuts", "seq", None)
    factor = P("seq", None, None)
    return jax.shard_map(
        on_device,
        mesh=mesh,
        in_specs=(placed, placed, placed, factor, factor),
        out_specs=(placed, placed, factor, factor),
        check_vma=False,
    )
```

```python
import functools

import jax
import jax.numpy as jnp
from jax import lax
from jax.experimental import pallas as pl
from jax.experimental.pallas import tpu as pltpu
from jax.sharding import PartitionSpec as P

MESH = pl.DeviceIdType.MESH
F32 = jnp.float32
BF16 = jnp.bfloat16
N = 64
OWN = 4
BLK = 256
D = 2048
ROWS = OWN * BLK
LANES = 512
VMEM_LIMIT = 50 * 1024 * 1024
NT = (((1,), (1,)), ((), ()))


def peer(me, step):
    turn, z = (step // 4) % 4, step % 4
    y = (z + turn) % 4
    core = me % 2
    flip = (step // 16 + z + turn) % 2
    to_z = (me // 16 + z + 2 * core) % 4
    to_y = (me // 2 + y + 2 * core) % 4
    rest = to_y * 2 + (core + flip) % 2
    return to_z * 16 + (me // 8) % 2 * 8 + rest, to_z * 8 + rest


def kernel(a_hbm, g_hbm, dy_hbm, l_hbm, r_hbm,
           a, dy, acc_left, acc_right, last,
           dz, left, right, left_t, expand, perm, sent, relay, got, sorted_, part, part_in,
           in_sem, send_sem, recv_sem, x_send, x_recv, cut_send, cut_recv, pair_in, rows_in, cut_in, all_in):
    cut = lax.axis_index("cuts")
    me = lax.axis_index("seq")
    other = 1 - cut
    half_d = D // 2

    my_x = (me // 8) % 2
    def tile_load(n):
        lanes = pl.ds(n * 256, 256)
        return pltpu.make_async_copy(a_hbm.at[:, lanes], a.at[:, lanes], in_sem.at[n])

    left_load = pltpu.make_async_copy(l_hbm, left, in_sem.at[4])
    tile_loads = [tile_load(n) for n in (0, 2, 1, 3)]
    hi = pl.ds(half_d, half_d)
    a_load = pltpu.make_async_copy(a_hbm.at[:, hi], a.at[:, hi], in_sem.at[5])
    other_loads = [
        pltpu.make_async_copy(r_hbm, right, in_sem.at[6]),
        pltpu.make_async_copy(dy_hbm, dy, in_sem.at[7]),
        pltpu.make_async_copy(g_hbm, dz, in_sem.at[8]),
    ]
    left_load.start()
    for load in tile_loads:
        load.start()

    near_side, lead = my_x == 0, me == 0
    partner = me + 8 - 16 * my_x
    my_place = (me // 16) * 8 + me % 8

    def tell(semaphore, to_cut, to):
        pl.semaphore_signal(semaphore, inc=1, device_id=(to_cut, to), device_id_type=MESH)

    def tell_rows(semaphore):
        def body(n, _):
            tell(semaphore, cut, (n // 8) * 16 + n % 8)
            return 0

        lax.fori_loop(1, N // 2, body, 0)

    barrier = pltpu.get_barrier_semaphore()

    @pl.when(near_side)
    def _():
        tell(barrier, cut, partner)

    @pl.when(lead)
    def _():
        tell(barrier, other, 0)
        tell_rows(barrier)

    @pl.when(my_x == 1)
    def _():
        pl.semaphore_wait(barrier, 1)
        tell(pair_in, cut, partner)

    def meet_partner():
        @pl.when(near_side)
        def _():
            pl.semaphore_wait(barrier, 1)
            pl.semaphore_wait(pair_in, 1)

            @pl.when(me != 0)
            def _():
                tell(rows_in, cut, 0)

    def meet_cut():
        @pl.when(lead)
        def _():
            pl.semaphore_wait(rows_in, N // 2 - 1)
            tell_rows(all_in)
            tell(cut_in, other, 0)

        @pl.when(me != 0)
        def _():
            pl.semaphore_wait(all_in, 1)

        @pl.when(near_side)
        def _():
            tell(all_in, cut, partner)

    def meet_other_cut():
        @pl.when(lead)
        def _():
            pl.semaphore_wait(cut_in, 1)
            tell_rows(all_in)

        @pl.when(me != 0)
        def _():
            pl.semaphore_wait(all_in, 1)

        @pl.when(near_side)
        def _():
            tell(all_in, cut, partner)

    rows = lax.broadcasted_iota(jnp.int32, (BLK, BLK), 0)
    cols = lax.broadcasted_iota(jnp.int32, (BLK, BLK), 1)

    def build_expand(which, half, x):
        factor = right if which else left
        own = (rows >> 1) & 3
        to = rows >> 3
        hit = cols == 4 * (16 * (to >> 3) + 8 * x + (to & 7)) + 2 * half + (rows & 1)
        for block in range(OWN):
            pick = jnp.where(hit & (own == block), 1.0, 0.0).astype(BF16)
            if which:
                out = lax.dot_general(pick, factor[block], NT, preferred_element_type=F32)
            else:
                out = jnp.dot(pick, factor[block], preferred_element_type=F32)
            expand[which, half, x, :, pl.ds(block * BLK, BLK)] = out.astype(BF16)

    def build_rest(which, skip):
        def body(n, _):
            half, x = n // 2, (my_x + 1 + n) % 2
            build_expand(which, half, x)
            return 0

        lax.fori_loop(skip, 4, body, 0)

    def compute_tile(which, q, x, tile):
        half, d0 = q // 2, (q % 2) * half_d
        source = dz if which else a
        outs = []
        for block in range(2):
            lanes = pl.ds(pl.multiple_of(d0 + block * LANES + tile * 256, 256), 256)
            out = jnp.dot(expand[which, half, x], source[:, lanes], preferred_element_type=F32)
            outs.append(out.reshape(32, 8, 256))
        out = jnp.concatenate(outs, axis=1).astype(BF16)
        sent[which, q, x, :, :, pl.ds(pl.multiple_of(tile * 256, 256), 256)] = out

    def compute(which, q, x):
        def body(tile, _):
            compute_tile(which, q, x, tile)
            return 0

        lax.fori_loop(0, LANES // 256, body, 0)

    def to_peers(which, q, source, origin):
        def body(step, _):
            to, place = peer(me, step)

            @pl.when(to != me)
            def _():
                pltpu.make_async_remote_copy(
                    src_ref=source.at[place], dst_ref=got.at[which, q, origin],
                    send_sem=send_sem.at[which, q], recv_sem=recv_sem.at[which, q],
                    device_id=(cut, to), device_id_type=MESH,
                ).start()

            return 0

        lax.fori_loop(0, N // 2, body, 0)

    def across(which, q, lanes=pl.ds(0, LANES)):
        return pltpu.make_async_remote_copy(
            src_ref=sent.at[which, q, 1 - my_x, :, :, lanes], dst_ref=relay.at[which, q, :, :, lanes],
            send_sem=x_send.at[which, q], recv_sem=x_recv.at[which, q],
            device_id=(cut, partner), device_id_type=MESH,
        )

    def send_near(which, q):
        to_peers(which, q, sent.at[which, q, my_x], me)
        got[which, q, me] = sent[which, q, my_x, my_place]

    def forward(which, q):
        to_peers(which, q, relay.at[which, q], partner)
        got[which, q, partner] = relay[which, q, my_place]

    def chunk(which, q):
        compute(which, q, 1 - my_x)
        across(which, q).start()
        compute(which, q, my_x)

    def all_of(which, q):
        span = pl.ds(0, N - 2)
        return pltpu.make_async_remote_copy(
            src_ref=got.at[which, q, span], dst_ref=got.at[which, q, span],
            send_sem=send_sem.at[which, q], recv_sem=recv_sem.at[which, q],
            device_id=(cut, me), device_id_type=MESH,
        )

    def receive(which, q):
        all_of(which, q).wait_recv()

        def sort(group, _):
            x = got[which, q, pl.ds(pl.multiple_of(group * 16, 16), 16)].reshape(BLK, LANES)
            y = jnp.dot(perm[...], x, preferred_element_type=F32).astype(BF16)
            sorted_[:, pl.ds(pl.multiple_of(group * 64, 64), 64), :] = y.reshape(4, 64, LANES)
            return 0

        lax.fori_loop(0, 4, sort, 0)

    def place_of(q, n):
        block, mine = n // 2, 2 * (q // 2) + n % 2
        lines = pl.ds(pl.multiple_of(mine * BLK, BLK), BLK)
        lanes = pl.ds(pl.multiple_of((q % 2) * half_d + block * LANES, LANES), LANES)
        return mine, lines, lanes

    def factor_gradient(which, q):
        def body(n, _):
            mine, lines, lanes = place_of(q, n)
            if which:
                acc_left[mine] += lax.dot_general(sorted_[n], a[lines, lanes], NT, preferred_element_type=F32)
            else:
                acc_right[mine] += lax.dot_general(dz[lines, lanes], sorted_[n], NT, preferred_element_type=F32)
            return 0

        lax.fori_loop(0, 4, body, 0)

    def row_gradient(which, q):
        def body(n, _):
            mine, lines, lanes = place_of(q, n)
            if which:
                a[lines, lanes] = jnp.dot(left_t[mine], sorted_[n], preferred_element_type=F32).astype(BF16)
            else:
                z = jnp.dot(right[mine], sorted_[n], preferred_element_type=F32)
                dy[lines, lanes] = (dy[lines, lanes].astype(F32) * z).astype(BF16)
            return 0

        lax.fori_loop(0, 4, body, 0)

    def exchange(which, half):
        return pltpu.make_async_remote_copy(
            src_ref=part.at[which, pl.ds(2 * half, 2)], dst_ref=part_in.at[which, pl.ds(2 * half, 2)],
            send_sem=cut_send.at[which, half], recv_sem=cut_recv.at[which, half],
            device_id=(other, me), device_id_type=MESH,
        )

    def hand_over(which, half):
        for block in (2 * half, 2 * half + 1):
            part[which, block] = (acc_left if which else acc_right)[block].astype(BF16)

    def finish(which, half):
        exchange(which, half).wait_recv()
        for block in (2 * half, 2 * half + 1):
            total = part[which, block].astype(F32) + part_in[which, block].astype(F32)
            if which:
                acc_left[block] = total
            else:
                acc_right[block] = total

    left_load.wait()
    build_expand(0, 0, 1 - my_x)
    meet_partner()
    for tile in range(2):
        tile_loads[2 * tile].wait()
        tile_loads[2 * tile + 1].wait()
        if tile == 1:
            a_load.start()
        compute_tile(0, 0, 1 - my_x, tile)
        across(0, 0, pl.ds(tile * 256, 256)).start()
    for load in other_loads:
        load.start()
    build_expand(0, 0, my_x)
    compute(0, 0, my_x)
    meet_cut()
    send_near(0, 0)
    a_load.wait()
    chunk(0, 1)
    send_near(0, 1)
    build_rest(0, 2)
    o_block, o_half, o_dev, o_own = rows >> 7, (rows >> 6) & 1, (rows >> 2) & 15, rows & 3
    perm[...] = jnp.where(cols == 16 * o_dev + 8 * o_block + 2 * o_own + o_half, 1.0, 0.0).astype(BF16)
    acc_left[...] = jnp.zeros_like(acc_left)
    acc_right[...] = jnp.zeros_like(acc_right)
    for q in (2, 3):
        chunk(0, q)
        send_near(0, q)

    other_loads[0].wait()
    build_rest(1, 0)
    other_loads[1].wait()
    other_loads[2].wait()

    def gate(n, _):
        lines = pl.ds(pl.multiple_of(n * 16, 16), 16)
        dz[lines, :] = (dy[lines, :].astype(F32) * dz[lines, :].astype(F32)).astype(BF16)
        return 0

    lax.fori_loop(0, ROWS // 16, gate, 0)
    eye = jnp.where(rows == cols, 1.0, 0.0).astype(BF16)
    for block in range(OWN):
        left_t[block] = lax.dot_general(eye, left[block], NT, preferred_element_type=F32).astype(BF16)

    def work(n):
        which, q = n // 4, n % 4
        receive(which, q)
        factor_gradient(which, q)
        if q % 2:
            hand_over(which, q // 2)
        row_gradient(which, q)

    for q in range(4):
        chunk(1, q)
        send_near(1, q)
        if q == 1:
            across(0, 0).wait_recv()
            forward(0, 0)
    meet_other_cut()
    across(0, 1).wait_recv()
    forward(0, 1)
    for n in range(2, 8):
        across(n // 4, n % 4).wait_recv()
        if n == 6:
            exchange(0, 0).start()
            exchange(0, 1).start()
        forward(n // 4, n % 4)
        work(n - 2)
    exchange(1, 0).start()
    work(6)
    receive(1, 3)
    factor_gradient(1, 3)
    last[0] = acc_left[2].astype(BF16)
    last[1] = acc_left[3].astype(BF16)
    row_gradient(1, 3)
    for n in range(3):
        finish(n // 2, n % 2)

    for which in range(2):
        for half in range(2 - which):
            exchange(which, half).wait_send()
        for q in range(4):
            all_of(which, q).wait_send()
            across(which, q).wait_send()


def write_out(gv, gg, gl, gr, gv_hbm, gg_hbm, gl_hbm, gr_hbm, sem):
    copies = []
    for n in range(OWN):
        lines = pl.ds(n * BLK, BLK)
        copies += [(gv.at[lines], gv_hbm.at[lines]), (gg.at[lines], gg_hbm.at[lines])]
        copies += [(gr.at[n], gr_hbm.at[n])]
    copies += [(gl.at[n], gl_hbm.at[n]) for n in range(OWN // 2)]
    copies = [pltpu.make_async_copy(src, dst, sem.at[n]) for n, (src, dst) in enumerate(copies)]
    for copy in copies:
        copy.start()
    for copy in copies:
        copy.wait()


def write_last(mine, other, gl_old, gl_hbm, total, sem):
    total[...] = mine[...].astype(F32) + other[...].astype(F32)
    copy = pltpu.make_async_copy(total, gl_hbm.at[pl.ds(OWN // 2, OWN // 2)], sem)
    copy.start()
    copy.wait()


def on_device(values_in, gate_out, grad_out, left_factor, right_factor):
    hbm = pl.BlockSpec(memory_space=pl.ANY)
    vmem = pl.BlockSpec(memory_space=pltpu.VMEM)
    dma = pltpu.SemaphoreType.DMA
    shapes = (((ROWS, D), BF16), ((ROWS, D), BF16), ((OWN, BLK, BLK), F32), ((OWN, BLK, BLK), F32))
    *held, last = pl.pallas_call(
        kernel,
        name="mixer_backward",
        out_shape=tuple(pltpu.VMEM(*shape) for shape in shapes) + (pltpu.VMEM((2, BLK, BLK), BF16),),
        in_specs=[hbm] * 5,
        out_specs=(vmem,) * 5,
        scratch_shapes=[
            pltpu.VMEM((ROWS, D), BF16),
            pltpu.VMEM((OWN, BLK, BLK), BF16),
            pltpu.VMEM((OWN, BLK, BLK), BF16),
            pltpu.VMEM((OWN, BLK, BLK), BF16),
            pltpu.VMEM((2, 2, 2, BLK, ROWS), BF16),
            pltpu.VMEM((BLK, BLK), BF16),
            pltpu.VMEM((2, 4, 2, N // 2, 16, LANES), BF16),
            pltpu.VMEM((2, 4, N // 2, 16, LANES), BF16),
            pltpu.VMEM((2, 4, N, 16, LANES), BF16),
            pltpu.VMEM((4, BLK, LANES), BF16),
            pltpu.VMEM((2, OWN, BLK, BLK), BF16),
            pltpu.VMEM((2, OWN, BLK, BLK), BF16),
            dma((9,)), dma((2, 4)), dma((2, 4)), dma((2, 4)), dma((2, 4)), dma((2, 2)), dma((2, 2)),
            *[pltpu.SemaphoreType.REGULAR] * 4,
        ],
        compiler_params=pltpu.CompilerParams(
            collective_id=0, has_side_effects=True, vmem_limit_bytes=VMEM_LIMIT
        ),
        cost_estimate=pl.CostEstimate(flops=28 * ROWS * BLK * D, bytes_accessed=14 << 20, transcendentals=0),
    )(
        values_in.reshape(ROWS, D), gate_out.reshape(ROWS, D), grad_out.reshape(ROWS, D),
        left_factor, right_factor,
    )
    arrived = lax.ppermute(last, "cuts", [(0, 1), (1, 0)])
    grad_values, grad_gate, grad_left, grad_right = pl.pallas_call(
        write_out,
        name="write_out",
        out_shape=tuple(jax.ShapeDtypeStruct(*shape) for shape in shapes),
        in_specs=[hbm] * 4,
        out_specs=(hbm,) * 4,
        scratch_shapes=[dma((4 * OWN,))],
        compiler_params=pltpu.CompilerParams(vmem_limit_bytes=1 << 20),
        cost_estimate=pl.CostEstimate(flops=0, bytes_accessed=10 << 20, transcendentals=0),
    )(*held)
    grad_left = pl.pallas_call(
        write_last,
        name="write_last",
        out_shape=jax.ShapeDtypeStruct(*shapes[2]),
        in_specs=[vmem, vmem, hbm],
        out_specs=hbm,
        scratch_shapes=[pltpu.VMEM((2, BLK, BLK), F32), dma],
        input_output_aliases={2: 0},
        compiler_params=pltpu.CompilerParams(vmem_limit_bytes=4 << 20),
        cost_estimate=pl.CostEstimate(flops=0, bytes_accessed=1 << 20, transcendentals=0),
    )(last, arrived, grad_left)
    return grad_values.reshape(1, ROWS, D), grad_gate.reshape(1, ROWS, D), grad_left, grad_right


def solution(mesh):
    placed = P("cuts", "seq", None)
    factor = P("seq", None, None)
    return jax.shard_map(
        on_device,
        mesh=mesh,
        in_specs=(placed, placed, placed, factor, factor),
        out_specs=(placed, placed, factor, factor),
        check_vma=False,
    )
```

```python
import functools

import jax
import jax.numpy as jnp
from jax import lax
from jax.experimental import pallas as pl
from jax.experimental.pallas import tpu as pltpu
from jax.sharding import PartitionSpec as P

MESH = pl.DeviceIdType.MESH
F32 = jnp.float32
BF16 = jnp.bfloat16
N = 64
OWN = 4
BLK = 256
D = 2048
ROWS = OWN * BLK
LANES = 512
VMEM_LIMIT = 46 * 1024 * 1024
NT = (((1,), (1,)), ((), ()))


def peer(me, step):
    turn, z = (step // 4) % 4, step % 4
    y = (z + turn) % 4
    core = me % 2
    flip = (step // 16 + z + turn) % 2
    to_z = (me // 16 + z + 2 * core) % 4
    to_y = (me // 2 + y + 2 * core) % 4
    rest = to_y * 2 + (core + flip) % 2
    return to_z * 16 + (me // 8) % 2 * 8 + rest, to_z * 8 + rest


def kernel(a_hbm, g_hbm, dy_hbm, l_hbm, r_hbm,
           a, dy, acc_left, acc_right, last, sorted_, left_t,
           dz, left, right, expand, perm, sent, relay, got, part, part_in,
           in_sem, send_sem, recv_sem, x_send, x_recv, cut_send, cut_recv, pair_in, rows_in, cut_in, all_in):
    cut = lax.axis_index("cuts")
    me = lax.axis_index("seq")
    other = 1 - cut
    half_d = D // 2

    my_x = (me // 8) % 2
    def tile_load(n):
        lanes = pl.ds(n * 256, 256)
        return pltpu.make_async_copy(a_hbm.at[:, lanes], a.at[:, lanes], in_sem.at[n])

    left_load = pltpu.make_async_copy(l_hbm, left, in_sem.at[4])
    tile_loads = [tile_load(n) for n in (0, 2, 1, 3)]
    hi = pl.ds(half_d, half_d)
    a_load = pltpu.make_async_copy(a_hbm.at[:, hi], a.at[:, hi], in_sem.at[5])
    other_loads = [
        pltpu.make_async_copy(r_hbm, right, in_sem.at[6]),
        pltpu.make_async_copy(dy_hbm, dy, in_sem.at[7]),
        pltpu.make_async_copy(g_hbm, dz, in_sem.at[8]),
    ]
    left_load.start()
    for load in tile_loads:
        load.start()

    near_side, lead = my_x == 0, me == 0
    partner = me + 8 - 16 * my_x
    my_place = (me // 16) * 8 + me % 8

    def tell(semaphore, to_cut, to):
        pl.semaphore_signal(semaphore, inc=1, device_id=(to_cut, to), device_id_type=MESH)

    def tell_rows(semaphore):
        def body(n, _):
            tell(semaphore, cut, (n // 8) * 16 + n % 8)
            return 0

        lax.fori_loop(1, N // 2, body, 0)

    barrier = pltpu.get_barrier_semaphore()

    @pl.when(near_side)
    def _():
        tell(barrier, cut, partner)

    @pl.when(lead)
    def _():
        tell(barrier, other, 0)
        tell_rows(barrier)

    @pl.when(my_x == 1)
    def _():
        pl.semaphore_wait(barrier, 1)
        tell(pair_in, cut, partner)

    def meet_partner():
        @pl.when(near_side)
        def _():
            pl.semaphore_wait(barrier, 1)
            pl.semaphore_wait(pair_in, 1)

            @pl.when(me != 0)
            def _():
                tell(rows_in, cut, 0)

    def meet_cut():
        @pl.when(lead)
        def _():
            pl.semaphore_wait(rows_in, N // 2 - 1)
            tell_rows(all_in)
            tell(cut_in, other, 0)

        @pl.when(me != 0)
        def _():
            pl.semaphore_wait(all_in, 1)

        @pl.when(near_side)
        def _():
            tell(all_in, cut, partner)

    def meet_other_cut():
        @pl.when(lead)
        def _():
            pl.semaphore_wait(cut_in, 1)
            tell_rows(all_in)

        @pl.when(me != 0)
        def _():
            pl.semaphore_wait(all_in, 1)

        @pl.when(near_side)
        def _():
            tell(all_in, cut, partner)

    rows = lax.broadcasted_iota(jnp.int32, (BLK, BLK), 0)
    cols = lax.broadcasted_iota(jnp.int32, (BLK, BLK), 1)

    def build_expand(which, half, x):
        factor = right if which else left
        own = (rows >> 1) & 3
        to = rows >> 3
        hit = cols == 4 * (16 * (to >> 3) + 8 * x + (to & 7)) + 2 * half + (rows & 1)
        for block in range(OWN):
            pick = jnp.where(hit & (own == block), 1.0, 0.0).astype(BF16)
            if which:
                out = lax.dot_general(pick, factor[block], NT, preferred_element_type=F32)
            else:
                out = jnp.dot(pick, factor[block], preferred_element_type=F32)
            expand[which, half, x, :, pl.ds(block * BLK, BLK)] = out.astype(BF16)

    def build_rest(which, skip):
        def body(n, _):
            half, x = n // 2, (my_x + 1 + n) % 2
            build_expand(which, half, x)
            return 0

        lax.fori_loop(skip, 4, body, 0)

    def compute_tile(which, q, x, tile):
        half, d0 = q // 2, (q % 2) * half_d
        source = dz if which else a
        outs = []
        for block in range(2):
            lanes = pl.ds(pl.multiple_of(d0 + block * LANES + tile * 256, 256), 256)
            out = jnp.dot(expand[which, half, x], source[:, lanes], preferred_element_type=F32)
            outs.append(out.reshape(32, 8, 256))
        out = jnp.concatenate(outs, axis=1).astype(BF16)
        sent[which, q, x, :, :, pl.ds(pl.multiple_of(tile * 256, 256), 256)] = out

    def compute(which, q, x):
        def body(tile, _):
            compute_tile(which, q, x, tile)
            return 0

        lax.fori_loop(0, LANES // 256, body, 0)

    def to_peers(which, q, source, origin):
        def body(step, _):
            to, place = peer(me, step)

            @pl.when(to != me)
            def _():
                pltpu.make_async_remote_copy(
                    src_ref=source.at[place], dst_ref=got.at[which, q, origin],
                    send_sem=send_sem.at[which, q], recv_sem=recv_sem.at[which, q],
                    device_id=(cut, to), device_id_type=MESH,
                ).start()

            return 0

        lax.fori_loop(0, N // 2, body, 0)

    def across(which, q, lanes=pl.ds(0, LANES)):
        return pltpu.make_async_remote_copy(
            src_ref=sent.at[which, q, 1 - my_x, :, :, lanes], dst_ref=relay.at[which, q, :, :, lanes],
            send_sem=x_send.at[which, q], recv_sem=x_recv.at[which, q],
            device_id=(cut, partner), device_id_type=MESH,
        )

    def send_near(which, q):
        to_peers(which, q, sent.at[which, q, my_x], me)
        got[which, q, me] = sent[which, q, my_x, my_place]

    def forward(which, q):
        to_peers(which, q, relay.at[which, q], partner)
        got[which, q, partner] = relay[which, q, my_place]

    def chunk(which, q):
        compute(which, q, 1 - my_x)
        across(which, q).start()
        compute(which, q, my_x)

    def all_of(which, q):
        span = pl.ds(0, N - 2)
        return pltpu.make_async_remote_copy(
            src_ref=got.at[which, q, span], dst_ref=got.at[which, q, span],
            send_sem=send_sem.at[which, q], recv_sem=recv_sem.at[which, q],
            device_id=(cut, me), device_id_type=MESH,
        )

    def receive(which, q):
        all_of(which, q).wait_recv()

        def sort(group, _):
            x = got[which, q, pl.ds(pl.multiple_of(group * 16, 16), 16)].reshape(BLK, LANES)
            y = jnp.dot(perm[...], x, preferred_element_type=F32).astype(BF16)
            sorted_[:, pl.ds(pl.multiple_of(group * 64, 64), 64), :] = y.reshape(4, 64, LANES)
            return 0

        lax.fori_loop(0, 4, sort, 0)

    def place_of(q, n):
        block, mine = n // 2, 2 * (q // 2) + n % 2
        lines = pl.ds(pl.multiple_of(mine * BLK, BLK), BLK)
        lanes = pl.ds(pl.multiple_of((q % 2) * half_d + block * LANES, LANES), LANES)
        return mine, lines, lanes

    def factor_gradient(which, q):
        def body(n, _):
            mine, lines, lanes = place_of(q, n)
            if which:
                acc_left[mine] += lax.dot_general(sorted_[n], a[lines, lanes], NT, preferred_element_type=F32)
            else:
                acc_right[mine] += lax.dot_general(dz[lines, lanes], sorted_[n], NT, preferred_element_type=F32)
            return 0

        lax.fori_loop(0, 4, body, 0)

    def row_gradient(which, q):
        def body(n, _):
            mine, lines, lanes = place_of(q, n)
            if which:
                a[lines, lanes] = jnp.dot(left_t[mine], sorted_[n], preferred_element_type=F32).astype(BF16)
            else:
                z = jnp.dot(right[mine], sorted_[n], preferred_element_type=F32)
                dy[lines, lanes] = (dy[lines, lanes].astype(F32) * z).astype(BF16)
            return 0

        lax.fori_loop(0, 4, body, 0)

    def exchange(which, half):
        return pltpu.make_async_remote_copy(
            src_ref=part.at[which, pl.ds(2 * half, 2)], dst_ref=part_in.at[which, pl.ds(2 * half, 2)],
            send_sem=cut_send.at[which, half], recv_sem=cut_recv.at[which, half],
            device_id=(other, me), device_id_type=MESH,
        )

    def hand_over(which, half):
        for block in (2 * half, 2 * half + 1):
            part[which, block] = (acc_left if which else acc_right)[block].astype(BF16)

    def finish(which, half):
        exchange(which, half).wait_recv()
        for block in (2 * half, 2 * half + 1):
            total = part[which, block].astype(F32) + part_in[which, block].astype(F32)
            if which:
                acc_left[block] = total
            else:
                acc_right[block] = total

    left_load.wait()
    build_expand(0, 0, 1 - my_x)
    meet_partner()
    for tile in range(2):
        tile_loads[2 * tile].wait()
        tile_loads[2 * tile + 1].wait()
        if tile == 1:
            a_load.start()
        compute_tile(0, 0, 1 - my_x, tile)
        across(0, 0, pl.ds(tile * 256, 256)).start()
    for load in other_loads:
        load.start()
    build_expand(0, 0, my_x)
    compute(0, 0, my_x)
    meet_cut()
    send_near(0, 0)
    a_load.wait()
    chunk(0, 1)
    send_near(0, 1)
    build_rest(0, 2)
    o_block, o_half, o_dev, o_own = rows >> 7, (rows >> 6) & 1, (rows >> 2) & 15, rows & 3
    perm[...] = jnp.where(cols == 16 * o_dev + 8 * o_block + 2 * o_own + o_half, 1.0, 0.0).astype(BF16)
    acc_left[...] = jnp.zeros_like(acc_left)
    acc_right[...] = jnp.zeros_like(acc_right)
    for q in (2, 3):
        chunk(0, q)
        send_near(0, q)

    other_loads[0].wait()
    build_rest(1, 0)
    other_loads[1].wait()
    other_loads[2].wait()

    def gate(n, _):
        lines = pl.ds(pl.multiple_of(n * 16, 16), 16)
        dz[lines, :] = (dy[lines, :].astype(F32) * dz[lines, :].astype(F32)).astype(BF16)
        return 0

    lax.fori_loop(0, ROWS // 16, gate, 0)
    eye = jnp.where(rows == cols, 1.0, 0.0).astype(BF16)
    for block in range(OWN):
        left_t[block] = lax.dot_general(eye, left[block], NT, preferred_element_type=F32).astype(BF16)

    def work(n):
        which, q = n // 4, n % 4
        receive(which, q)
        factor_gradient(which, q)
        if q % 2:
            hand_over(which, q // 2)
            if n == 5:
                exchange(1, 0).start()
        row_gradient(which, q)

    for q in range(4):
        chunk(1, q)
        send_near(1, q)
        if q == 1:
            across(0, 0).wait_recv()
            forward(0, 0)
    meet_other_cut()
    across(0, 1).wait_recv()
    forward(0, 1)
    for n in range(2, 8):
        across(n // 4, n % 4).wait_recv()
        if n == 6:
            exchange(0, 0).start()
            exchange(0, 1).start()
        forward(n // 4, n % 4)
        work(n - 2)
    work(6)
    receive(1, 3)
    factor_gradient(1, 3)
    last[0] = acc_left[2].astype(BF16)
    last[1] = acc_left[3].astype(BF16)
    for n in range(3):
        finish(n // 2, n % 2)

    for which in range(2):
        for half in range(2 - which):
            exchange(which, half).wait_send()
        for q in range(4):
            all_of(which, q).wait_send()
            across(which, q).wait_send()


def write_out(gv, gg, gl, gr, y, left_t, gv_hbm, gg_hbm, gl_hbm, gr_hbm, tail, sem):
    copies = [(gg.at[pl.ds(n * BLK, BLK)], gg_hbm.at[pl.ds(n * BLK, BLK)]) for n in range(OWN)]
    copies += [(gv.at[pl.ds(n * BLK, BLK)], gv_hbm.at[pl.ds(n * BLK, BLK)]) for n in range(OWN // 2)]
    early = (pl.ds(ROWS // 2, ROWS // 2), pl.ds(0, D // 2))
    copies += [(gv.at[early], gv_hbm.at[early])]
    copies += [(gr.at[n], gr_hbm.at[n]) for n in range(OWN)]
    copies += [(gl.at[n], gl_hbm.at[n]) for n in range(OWN // 2)]
    first = len(copies)
    copies = [pltpu.make_async_copy(src, dst, sem.at[n]) for n, (src, dst) in enumerate(copies)]
    for copy in copies:
        copy.start()
    for n in range(4):
        mine = OWN // 2 + n % 2
        tail[n] = jnp.dot(left_t[mine], y[n], preferred_element_type=F32).astype(BF16)
        place = (pl.ds(mine * BLK, BLK), pl.ds(D // 2 + n // 2 * LANES, LANES))
        copies.append(pltpu.make_async_copy(tail.at[n], gv_hbm.at[place], sem.at[first + n]))
        copies[-1].start()
    for copy in copies:
        copy.wait()


def write_last(mine, other, gl_old, gl_hbm, total, sem):
    total[...] = mine[...].astype(F32) + other[...].astype(F32)
    copy = pltpu.make_async_copy(total, gl_hbm.at[pl.ds(OWN // 2, OWN // 2)], sem)
    copy.start()
    copy.wait()


def on_device(values_in, gate_out, grad_out, left_factor, right_factor):
    hbm = pl.BlockSpec(memory_space=pl.ANY)
    vmem = pl.BlockSpec(memory_space=pltpu.VMEM)
    dma = pltpu.SemaphoreType.DMA
    shapes = (((ROWS, D), BF16), ((ROWS, D), BF16), ((OWN, BLK, BLK), F32), ((OWN, BLK, BLK), F32))
    *held, last, last_rows, left_t = pl.pallas_call(
        kernel,
        name="mixer_backward",
        out_shape=tuple(pltpu.VMEM(*shape) for shape in shapes) + (
            pltpu.VMEM((2, BLK, BLK), BF16), pltpu.VMEM((4, BLK, LANES), BF16), pltpu.VMEM((OWN, BLK, BLK), BF16),
        ),
        in_specs=[hbm] * 5,
        out_specs=(vmem,) * 7,
        scratch_shapes=[
            pltpu.VMEM((ROWS, D), BF16),
            pltpu.VMEM((OWN, BLK, BLK), BF16),
            pltpu.VMEM((OWN, BLK, BLK), BF16),
            pltpu.VMEM((2, 2, 2, BLK, ROWS), BF16),
            pltpu.VMEM((BLK, BLK), BF16),
            pltpu.VMEM((2, 4, 2, N // 2, 16, LANES), BF16),
            pltpu.VMEM((2, 4, N // 2, 16, LANES), BF16),
            pltpu.VMEM((2, 4, N, 16, LANES), BF16),
            pltpu.VMEM((2, OWN, BLK, BLK), BF16),
            pltpu.VMEM((2, OWN, BLK, BLK), BF16),
            dma((9,)), dma((2, 4)), dma((2, 4)), dma((2, 4)), dma((2, 4)), dma((2, 2)), dma((2, 2)),
            *[pltpu.SemaphoreType.REGULAR] * 4,
        ],
        compiler_params=pltpu.CompilerParams(
            collective_id=0, has_side_effects=True, vmem_limit_bytes=VMEM_LIMIT
        ),
        cost_estimate=pl.CostEstimate(flops=28 * ROWS * BLK * D, bytes_accessed=14 << 20, transcendentals=0),
    )(
        values_in.reshape(ROWS, D), gate_out.reshape(ROWS, D), grad_out.reshape(ROWS, D),
        left_factor, right_factor,
    )
    arrived = lax.ppermute(last, "cuts", [(0, 1), (1, 0)])
    grad_values, grad_gate, grad_left, grad_right = pl.pallas_call(
        write_out,
        name="write_out",
        out_shape=tuple(jax.ShapeDtypeStruct(*shape) for shape in shapes),
        in_specs=[hbm] * 4 + [vmem] * 2,
        out_specs=(hbm,) * 4,
        scratch_shapes=[pltpu.VMEM((4, BLK, LANES), BF16), dma((5 * OWN,))],
        compiler_params=pltpu.CompilerParams(vmem_limit_bytes=8 << 20),
        cost_estimate=pl.CostEstimate(flops=0, bytes_accessed=10 << 20, transcendentals=0),
    )(*held, last_rows, left_t)
    grad_left = pl.pallas_call(
        write_last,
        name="write_last",
        out_shape=jax.ShapeDtypeStruct(*shapes[2]),
        in_specs=[vmem, vmem, hbm],
        out_specs=hbm,
        scratch_shapes=[pltpu.VMEM((2, BLK, BLK), F32), dma],
        input_output_aliases={2: 0},
        compiler_params=pltpu.CompilerParams(vmem_limit_bytes=4 << 20),
        cost_estimate=pl.CostEstimate(flops=0, bytes_accessed=1 << 20, transcendentals=0),
    )(last, arrived, grad_left)
    return grad_values.reshape(1, ROWS, D), grad_gate.reshape(1, ROWS, D), grad_left, grad_right


def solution(mesh):
    placed = P("cuts", "seq", None)
    factor = P("seq", None, None)
    return jax.shard_map(
        on_device,
        mesh=mesh,
        in_specs=(placed, placed, placed, factor, factor),
        out_specs=(placed, placed, factor, factor),
        check_vma=False,
    )
```

```python
import functools

import jax
import jax.numpy as jnp
from jax import lax
from jax.experimental import pallas as pl
from jax.experimental.pallas import tpu as pltpu
from jax.sharding import PartitionSpec as P

MESH = pl.DeviceIdType.MESH
F32 = jnp.float32
BF16 = jnp.bfloat16
N = 64
OWN = 4
BLK = 256
D = 2048
ROWS = OWN * BLK
LANES = 512
VMEM_LIMIT = 50 * 1024 * 1024
NT = (((1,), (1,)), ((), ()))


def peer(me, step):
    turn, z = (step // 4) % 4, step % 4
    y = (z + turn) % 4
    core = me % 2
    flip = (step // 16 + z + turn) % 2
    to_z = (me // 16 + z + 2 * core) % 4
    to_y = (me // 2 + y + 2 * core) % 4
    rest = to_y * 2 + (core + flip) % 2
    return to_z * 16 + (me // 8) % 2 * 8 + rest, to_z * 8 + rest


def kernel(a_hbm, g_hbm, dy_hbm, l_hbm, r_hbm,
           a, dy, acc_left, acc_right, last,
           dz, left, right, left_t, expand, perm, sent, relay, got, sorted_, part, part_in,
           in_sem, send_sem, recv_sem, x_send, x_recv, cut_send, cut_recv, pair_in, rows_in, cut_in, all_in):
    cut = lax.axis_index("cuts")
    me = lax.axis_index("seq")
    other = 1 - cut
    half_d = D // 2

    my_x = (me // 8) % 2
    def tile_load(n):
        lanes = pl.ds(n * 256, 256)
        return pltpu.make_async_copy(a_hbm.at[:, lanes], a.at[:, lanes], in_sem.at[n])

    left_load = pltpu.make_async_copy(l_hbm, left, in_sem.at[4])
    tile_loads = [tile_load(n) for n in (0, 2, 1, 3)]
    hi = pl.ds(half_d, half_d)
    a_load = pltpu.make_async_copy(a_hbm.at[:, hi], a.at[:, hi], in_sem.at[5])
    other_loads = [
        pltpu.make_async_copy(r_hbm, right, in_sem.at[6]),
        pltpu.make_async_copy(dy_hbm, dy, in_sem.at[7]),
        pltpu.make_async_copy(g_hbm, dz, in_sem.at[8]),
    ]
    left_load.start()
    for load in tile_loads:
        load.start()

    near_side, lead = my_x == 0, me == 0
    partner = me + 8 - 16 * my_x
    my_place = (me // 16) * 8 + me % 8

    def tell(semaphore, to_cut, to):
        pl.semaphore_signal(semaphore, inc=1, device_id=(to_cut, to), device_id_type=MESH)

    def tell_rows(semaphore):
        def body(n, _):
            tell(semaphore, cut, (n // 8) * 16 + n % 8)
            return 0

        lax.fori_loop(1, N // 2, body, 0)

    barrier = pltpu.get_barrier_semaphore()

    @pl.when(near_side)
    def _():
        tell(barrier, cut, partner)

    @pl.when(lead)
    def _():
        tell(barrier, other, 0)
        tell_rows(barrier)

    @pl.when(my_x == 1)
    def _():
        pl.semaphore_wait(barrier, 1)
        tell(pair_in, cut, partner)

    def meet_partner():
        @pl.when(near_side)
        def _():
            pl.semaphore_wait(barrier, 1)
            pl.semaphore_wait(pair_in, 1)

            @pl.when(me != 0)
            def _():
                tell(rows_in, cut, 0)

    def meet_cut():
        @pl.when(lead)
        def _():
            pl.semaphore_wait(rows_in, N // 2 - 1)
            tell_rows(all_in)
            tell(cut_in, other, 0)

        @pl.when(me != 0)
        def _():
            pl.semaphore_wait(all_in, 1)

        @pl.when(near_side)
        def _():
            tell(all_in, cut, partner)

    def meet_other_cut():
        @pl.when(lead)
        def _():
            pl.semaphore_wait(cut_in, 1)
            tell_rows(all_in)

        @pl.when(me != 0)
        def _():
            pl.semaphore_wait(all_in, 1)

        @pl.when(near_side)
        def _():
            tell(all_in, cut, partner)

    rows = lax.broadcasted_iota(jnp.int32, (BLK, BLK), 0)
    cols = lax.broadcasted_iota(jnp.int32, (BLK, BLK), 1)

    def pick_of(half, x, block):
        to = rows >> 3
        hit = cols == 4 * (16 * (to >> 3) + 8 * x + (to & 7)) + 2 * half + (rows & 1)
        return jnp.where(hit & (((rows >> 1) & 3) == block), 1.0, 0.0).astype(BF16)

    def build_expand(which, half, x):
        factor = right if which else left
        own = (rows >> 1) & 3
        to = rows >> 3
        hit = cols == 4 * (16 * (to >> 3) + 8 * x + (to & 7)) + 2 * half + (rows & 1)
        for block in range(OWN):
            pick = jnp.where(hit & (own == block), 1.0, 0.0).astype(BF16)
            if which:
                out = lax.dot_general(pick, factor[block], NT, preferred_element_type=F32)
            else:
                out = jnp.dot(pick, factor[block], preferred_element_type=F32)
            expand[which, half, x, :, pl.ds(block * BLK, BLK)] = out.astype(BF16)

    def build_rest(which, skip):
        def body(n, _):
            half, x = n // 2, (my_x + 1 + n) % 2
            build_expand(which, half, x)
            return 0

        lax.fori_loop(skip, 4, body, 0)

    def compute_tile(which, q, x, tile):
        half, d0 = q // 2, (q % 2) * half_d
        source = dz if which else a
        outs = []
        for block in range(2):
            lanes = pl.ds(pl.multiple_of(d0 + block * LANES + tile * 256, 256), 256)
            out = jnp.dot(expand[which, half, x], source[:, lanes], preferred_element_type=F32)
            outs.append(out.reshape(32, 8, 256))
        out = jnp.concatenate(outs, axis=1).astype(BF16)
        sent[which, q, x, :, :, pl.ds(pl.multiple_of(tile * 256, 256), 256)] = out

    def compute(which, q, x):
        def body(tile, _):
            compute_tile(which, q, x, tile)
            return 0

        lax.fori_loop(0, LANES // 256, body, 0)

    def to_peers(which, q, source, origin):
        def body(step, _):
            to, place = peer(me, step)

            @pl.when(to != me)
            def _():
                pltpu.make_async_remote_copy(
                    src_ref=source.at[place], dst_ref=got.at[which, q, origin],
                    send_sem=send_sem.at[which, q], recv_sem=recv_sem.at[which, q],
                    device_id=(cut, to), device_id_type=MESH,
                ).start()

            return 0

        lax.fori_loop(0, N // 2, body, 0)

    def across(which, q, lanes=pl.ds(0, LANES)):
        return pltpu.make_async_remote_copy(
            src_ref=sent.at[which, q, 1 - my_x, :, :, lanes], dst_ref=relay.at[which, q, :, :, lanes],
            send_sem=x_send.at[which, q], recv_sem=x_recv.at[which, q],
            device_id=(cut, partner), device_id_type=MESH,
        )

    def send_near(which, q):
        to_peers(which, q, sent.at[which, q, my_x], me)
        got[which, q, me] = sent[which, q, my_x, my_place]

    def forward(which, q):
        to_peers(which, q, relay.at[which, q], partner)
        got[which, q, partner] = relay[which, q, my_place]

    def chunk(which, q):
        compute(which, q, 1 - my_x)
        across(which, q).start()
        compute(which, q, my_x)

    def all_of(which, q):
        span = pl.ds(0, N - 2)
        return pltpu.make_async_remote_copy(
            src_ref=got.at[which, q, span], dst_ref=got.at[which, q, span],
            send_sem=send_sem.at[which, q], recv_sem=recv_sem.at[which, q],
            device_id=(cut, me), device_id_type=MESH,
        )

    def receive(which, q):
        all_of(which, q).wait_recv()

        def sort(group, _):
            x = got[which, q, pl.ds(pl.multiple_of(group * 16, 16), 16)].reshape(BLK, LANES)
            y = jnp.dot(perm[...], x, preferred_element_type=F32).astype(BF16)
            sorted_[:, pl.ds(pl.multiple_of(group * 64, 64), 64), :] = y.reshape(4, 64, LANES)
            return 0

        lax.fori_loop(0, 4, sort, 0)

    def place_of(q, n):
        block, mine = n // 2, 2 * (q // 2) + n % 2
        lines = pl.ds(pl.multiple_of(mine * BLK, BLK), BLK)
        lanes = pl.ds(pl.multiple_of((q % 2) * half_d + block * LANES, LANES), LANES)
        return mine, lines, lanes

    def factor_gradient(which, q):
        def body(n, _):
            mine, lines, lanes = place_of(q, n)
            if which:
                acc_left[mine] += lax.dot_general(sorted_[n], a[lines, lanes], NT, preferred_element_type=F32)
            else:
                acc_right[mine] += lax.dot_general(dz[lines, lanes], sorted_[n], NT, preferred_element_type=F32)
            return 0

        lax.fori_loop(0, 4, body, 0)

    def row_gradient(which, q):
        def body(n, _):
            mine, lines, lanes = place_of(q, n)
            if which:
                a[lines, lanes] = jnp.dot(left_t[mine], sorted_[n], preferred_element_type=F32).astype(BF16)
            else:
                z = jnp.dot(right[mine], sorted_[n], preferred_element_type=F32)
                dy[lines, lanes] = (dy[lines, lanes].astype(F32) * z).astype(BF16)
            return 0

        lax.fori_loop(0, 4, body, 0)

    def exchange(which, half):
        return pltpu.make_async_remote_copy(
            src_ref=part.at[which, pl.ds(2 * half, 2)], dst_ref=part_in.at[which, pl.ds(2 * half, 2)],
            send_sem=cut_send.at[which, half], recv_sem=cut_recv.at[which, half],
            device_id=(other, me), device_id_type=MESH,
        )

    def hand_over(which, half):
        for block in (2 * half, 2 * half + 1):
            part[which, block] = (acc_left if which else acc_right)[block].astype(BF16)

    def finish(which, half):
        exchange(which, half).wait_recv()
        for block in (2 * half, 2 * half + 1):
            total = part[which, block].astype(F32) + part_in[which, block].astype(F32)
            if which:
                acc_left[block] = total
            else:
                acc_right[block] = total

    for block in range(OWN):
        sorted_[block, :, pl.ds(0, BLK)] = pick_of(0, 1 - my_x, block)
    left_load.wait()
    for block in range(OWN):
        out = jnp.dot(sorted_[block, :, pl.ds(0, BLK)], left[block], preferred_element_type=F32)
        expand[0, 0, 1 - my_x, :, pl.ds(block * BLK, BLK)] = out.astype(BF16)
    meet_partner()
    for tile in range(2):
        tile_loads[2 * tile].wait()
        tile_loads[2 * tile + 1].wait()
        if tile == 1:
            a_load.start()
        compute_tile(0, 0, 1 - my_x, tile)
        across(0, 0, pl.ds(tile * 256, 256)).start()
    for load in other_loads:
        load.start()
    build_expand(0, 0, my_x)
    compute(0, 0, my_x)
    meet_cut()
    send_near(0, 0)
    a_load.wait()
    chunk(0, 1)
    send_near(0, 1)
    build_rest(0, 2)
    o_block, o_half, o_dev, o_own = rows >> 7, (rows >> 6) & 1, (rows >> 2) & 15, rows & 3
    perm[...] = jnp.where(cols == 16 * o_dev + 8 * o_block + 2 * o_own + o_half, 1.0, 0.0).astype(BF16)
    acc_left[...] = jnp.zeros_like(acc_left)
    acc_right[...] = jnp.zeros_like(acc_right)
    for q in (2, 3):
        chunk(0, q)
        send_near(0, q)

    other_loads[0].wait()
    build_rest(1, 0)
    other_loads[1].wait()
    other_loads[2].wait()

    def gate(n, _):
        lines = pl.ds(pl.multiple_of(n * 16, 16), 16)
        dz[lines, :] = (dy[lines, :].astype(F32) * dz[lines, :].astype(F32)).astype(BF16)
        return 0

    lax.fori_loop(0, ROWS // 16, gate, 0)
    eye = jnp.where(rows == cols, 1.0, 0.0).astype(BF16)
    for block in range(OWN):
        left_t[block] = lax.dot_general(eye, left[block], NT, preferred_element_type=F32).astype(BF16)

    def work(n):
        which, q = n // 4, n % 4
        receive(which, q)
        factor_gradient(which, q)
        if q % 2:
            hand_over(which, q // 2)
        row_gradient(which, q)

    for q in range(4):
        chunk(1, q)
        send_near(1, q)
        if q == 1:
            across(0, 0).wait_recv()
            forward(0, 0)
    meet_other_cut()
    across(0, 1).wait_recv()
    forward(0, 1)
    for n in range(2, 8):
        across(n // 4, n % 4).wait_recv()
        if n == 6:
            exchange(0, 0).start()
            exchange(0, 1).start()
        forward(n // 4, n % 4)
        work(n - 2)
    exchange(1, 0).start()
    work(6)
    receive(1, 3)
    factor_gradient(1, 3)
    last[0] = acc_left[2].astype(BF16)
    last[1] = acc_left[3].astype(BF16)
    row_gradient(1, 3)
    for n in range(3):
        finish(n // 2, n % 2)

    for which in range(2):
        for half in range(2 - which):
            exchange(which, half).wait_send()
        for q in range(4):
            all_of(which, q).wait_send()
            across(which, q).wait_send()


def write_out(gv, gg, gl, gr, gv_hbm, gg_hbm, gl_hbm, gr_hbm, sem):
    copies = []
    for n in range(OWN):
        lines = pl.ds(n * BLK, BLK)
        copies += [(gv.at[lines], gv_hbm.at[lines]), (gg.at[lines], gg_hbm.at[lines])]
        copies += [(gr.at[n], gr_hbm.at[n])]
    copies += [(gl.at[n], gl_hbm.at[n]) for n in range(OWN // 2)]
    copies = [pltpu.make_async_copy(src, dst, sem.at[n]) for n, (src, dst) in enumerate(copies)]
    for copy in copies:
        copy.start()
    for copy in copies:
        copy.wait()


def write_last(mine, other, gl_old, gl_hbm, total, sem):
    total[...] = mine[...].astype(F32) + other[...].astype(F32)
    copy = pltpu.make_async_copy(total, gl_hbm.at[pl.ds(OWN // 2, OWN // 2)], sem)
    copy.start()
    copy.wait()


def on_device(values_in, gate_out, grad_out, left_factor, right_factor):
    hbm = pl.BlockSpec(memory_space=pl.ANY)
    vmem = pl.BlockSpec(memory_space=pltpu.VMEM)
    dma = pltpu.SemaphoreType.DMA
    shapes = (((ROWS, D), BF16), ((ROWS, D), BF16), ((OWN, BLK, BLK), F32), ((OWN, BLK, BLK), F32))
    *held, last = pl.pallas_call(
        kernel,
        name="mixer_backward",
        out_shape=tuple(pltpu.VMEM(*shape) for shape in shapes) + (pltpu.VMEM((2, BLK, BLK), BF16),),
        in_specs=[hbm] * 5,
        out_specs=(vmem,) * 5,
        scratch_shapes=[
            pltpu.VMEM((ROWS, D), BF16),
            pltpu.VMEM((OWN, BLK, BLK), BF16),
            pltpu.VMEM((OWN, BLK, BLK), BF16),
            pltpu.VMEM((OWN, BLK, BLK), BF16),
            pltpu.VMEM((2, 2, 2, BLK, ROWS), BF16),
            pltpu.VMEM((BLK, BLK), BF16),
            pltpu.VMEM((2, 4, 2, N // 2, 16, LANES), BF16),
            pltpu.VMEM((2, 4, N // 2, 16, LANES), BF16),
            pltpu.VMEM((2, 4, N, 16, LANES), BF16),
            pltpu.VMEM((4, BLK, LANES), BF16),
            pltpu.VMEM((2, OWN, BLK, BLK), BF16),
            pltpu.VMEM((2, OWN, BLK, BLK), BF16),
            dma((9,)), dma((2, 4)), dma((2, 4)), dma((2, 4)), dma((2, 4)), dma((2, 2)), dma((2, 2)),
            *[pltpu.SemaphoreType.REGULAR] * 4,
        ],
        compiler_params=pltpu.CompilerParams(
            collective_id=0, has_side_effects=True, vmem_limit_bytes=VMEM_LIMIT
        ),
        cost_estimate=pl.CostEstimate(flops=28 * ROWS * BLK * D, bytes_accessed=14 << 20, transcendentals=0),
    )(
        values_in.reshape(ROWS, D), gate_out.reshape(ROWS, D), grad_out.reshape(ROWS, D),
        left_factor, right_factor,
    )
    arrived = lax.ppermute(last, "cuts", [(0, 1), (1, 0)])
    grad_values, grad_gate, grad_left, grad_right = pl.pallas_call(
        write_out,
        name="write_out",
        out_shape=tuple(jax.ShapeDtypeStruct(*shape) for shape in shapes),
        in_specs=[hbm] * 4,
        out_specs=(hbm,) * 4,
        scratch_shapes=[dma((4 * OWN,))],
        compiler_params=pltpu.CompilerParams(vmem_limit_bytes=1 << 20),
        cost_estimate=pl.CostEstimate(flops=0, bytes_accessed=10 << 20, transcendentals=0),
    )(*held)
    grad_left = pl.pallas_call(
        write_last,
        name="write_last",
        out_shape=jax.ShapeDtypeStruct(*shapes[2]),
        in_specs=[vmem, vmem, hbm],
        out_specs=hbm,
        scratch_shapes=[pltpu.VMEM((2, BLK, BLK), F32), dma],
        input_output_aliases={2: 0},
        compiler_params=pltpu.CompilerParams(vmem_limit_bytes=4 << 20),
        cost_estimate=pl.CostEstimate(flops=0, bytes_accessed=1 << 20, transcendentals=0),
    )(last, arrived, grad_left)
    return grad_values.reshape(1, ROWS, D), grad_gate.reshape(1, ROWS, D), grad_left, grad_right


def solution(mesh):
    placed = P("cuts", "seq", None)
    factor = P("seq", None, None)
    return jax.shard_map(
        on_device,
        mesh=mesh,
        in_specs=(placed, placed, placed, factor, factor),
        out_specs=(placed, placed, factor, factor),
        check_vma=False,
    )
```
